32 devices in a mesh: segment: 2 (over core), space: 16 (over z, y, x).
Axes of the slice: x: 2, y: 2, z: 4, core: 2. Of those that a mesh axis runs over, the one named last changes fastest.
Arguments:
- stash_down: bfloat16 [2, 64, 32, 384], P('segment', 'space'), may hold values from -6 to 6
- stash_up: bfloat16 [2, 64, 32, 384], P('segment', 'space'), may hold values from -6 to 6
- grad_down: bfloat16 [64, 32, 384], P('space'), may hold values from -6 to 6
- grad_up: bfloat16 [64, 32, 384], P('space'), may hold values from -6 to 6
- dw_kernel: bfloat16 [2, 2, 49, 384], P('segment'), as said below
- norm_gain: float32 [2, 2, 384], P('segment'), as said below
- norm_bias: float32 [2, 2, 384], P('segment'), as said below
- w_in: bfloat16 [2, 2, 384, 1536], P('segment', None, 'space'), as said below
- b_in: float32 [2, 2, 1536], P('segment'), as said below
- w_out: bfloat16 [2, 2, 1536, 384], P('segment', None, 'space'), as said below
- layer_scale: float32 [2, 2, 384], P('segment'), as said below
Outputs:
- input_grad_down: bfloat16 [2, 64, 32, 384], P('segment', 'space')
- input_grad_up: bfloat16 [2, 64, 32, 384], P('segment', 'space')
- w_out_grad: float32 [2, 1536, 384], P('segment', 'space')
- kernel_grad: float32 [2, 49, 384], P('segment')
The draws below stay inside these ranges and needn't reach their ends.
Inputs may be any that keep to these rules, and one draw needn't show every extreme that they name: `dw_kernel`: entry [s, 1] equals entry [1 - s, 0] for every s. `norm_gain`: entry [s, 1] equals entry [1 - s, 0] for every s. `norm_bias`: entry [s, 1] equals entry [1 - s, 0] for every s. `w_in`: entry [s, 1] equals entry [1 - s, 0] for every s. `b_in`: entry [s, 1] equals entry [1 - s, 0] for every s. `w_out`: entry [s, 1] equals entry [1 - s, 0] for every s. `layer_scale`: entry [s, 1] equals entry [1 - s, 0] for every s.
All inputs are finite; a program needn't handle non-finite values.
Results may differ from the reference program's by a relative error of at most 0.0075.
Values may be sent and summed in bfloat16 or wider, within the bound.
A program may use at most 64 MiB of HBM per device.

```python
import math
import jax
import jax.numpy as jnp
from jax import lax

D = 384
HID = 1536
KSIDE = 7
COLS = 32
H_ROWS = 64
N_SEGMENT = 2


def mirrored(base):
    return jnp.stack([base, base[::-1]], axis=1)


def bounded(key, shape):
    return jax.random.truncated_normal(key, -4.0, 4.0, shape, jnp.float32)


def draw_dw_kernel(key, part):
    base = bounded(jax.random.fold_in(key, 11), (N_SEGMENT, KSIDE * KSIDE, D)) / KSIDE
    return mirrored(base).astype(jnp.bfloat16)


def draw_norm_gain(key, part):
    base = 1.0 + 0.1 * bounded(jax.random.fold_in(key, 12), (N_SEGMENT, D))
    return mirrored(base)


def draw_norm_bias(key, part):
    base = 0.5 * bounded(jax.random.fold_in(key, 13), (N_SEGMENT, D))
    return mirrored(base)


def draw_w_in(key, part):
    base = bounded(jax.random.fold_in(key, 14), (N_SEGMENT, D, HID)) / jnp.sqrt(jnp.float32(D))
    return mirrored(base).astype(jnp.bfloat16)


def draw_b_in(key, part):
    base = 0.5 * bounded(jax.random.fold_in(key, 15), (N_SEGMENT, HID))
    return mirrored(base)


def draw_w_out(key, part):
    base = bounded(jax.random.fold_in(key, 16), (N_SEGMENT, HID, D)) / jnp.sqrt(jnp.float32(HID))
    return mirrored(base).astype(jnp.bfloat16)


def draw_layer_scale(key, part):
    low = jnp.log(jnp.float32(0.1))
    high = jnp.log(jnp.float32(0.6))
    base = jnp.exp(jax.random.uniform(jax.random.fold_in(key, 17), (N_SEGMENT, D), jnp.float32, low, high))
    return mirrored(base)


def block_scale(rng, extent, split, smallest, top_value):
    factor_of = 1.0
    for position, blocks in split:
        heights = jax.random.uniform(jax.random.fold_in(jax.random.fold_in(rng, 6), position), (blocks,), jnp.float32, smallest / len(split), top_value / len(split))
        factor_of = factor_of * jnp.repeat(jnp.exp(heights), extent[position] // blocks).reshape((-1,) + (1,) * (len(extent) - 1 - position))
    return factor_of


def normal_values(own_key, shape, spread, reach, split=(), dtype=jnp.bfloat16):
    drawn = spread * jax.random.normal(own_key, shape, jnp.float32)
    if split:
        drawn = drawn * block_scale(own_key, shape, split, -0.22, 0.18)
    return jnp.clip(drawn, -reach, reach).astype(dtype)


def setup_inputs(seed: int = 0) -> dict:
    keys = jax.random.split(jax.random.key(seed), 12)
    stash_down = normal_values(keys[0], (N_SEGMENT, H_ROWS, COLS, D), 1.0, 6.0, ((0, 2), (1, 16)))
    stash_up = normal_values(keys[1], (N_SEGMENT, H_ROWS, COLS, D), 1.0, 6.0, ((0, 2), (1, 16)))
    grad_down = normal_values(keys[2], (H_ROWS, COLS, D), 1.0, 6.0, ((0, 16),))
    grad_up = normal_values(keys[3], (H_ROWS, COLS, D), 1.0, 6.0, ((0, 16),))
    dw_kernel = draw_dw_kernel(jax.random.fold_in(keys[11], 71), 0)
    norm_gain = draw_norm_gain(jax.random.fold_in(keys[11], 71), 0)
    norm_bias = draw_norm_bias(jax.random.fold_in(keys[11], 71), 0)
    w_in = draw_w_in(jax.random.fold_in(keys[11], 71), 0)
    b_in = draw_b_in(jax.random.fold_in(keys[11], 71), 0)
    w_out = draw_w_out(jax.random.fold_in(keys[11], 71), 0)
    layer_scale = draw_layer_scale(jax.random.fold_in(keys[11], 71), 0)
    return {"stash_down": stash_down, "stash_up": stash_up, "grad_down": grad_down, "grad_up": grad_up, "dw_kernel": dw_kernel, "norm_gain": norm_gain, "norm_bias": norm_bias, "w_in": w_in, "b_in": b_in, "w_out": w_out, "layer_scale": layer_scale}


def gelu_parts(a):
    inner = 0.7978845608 * (a + 0.044715 * a * a * a)
    th = jnp.tanh(inner)
    value = 0.5 * a * (1.0 + th)
    slope = 0.5 * (1.0 + th) + 0.5 * a * (1.0 - th * th) * 0.7978845608 * (1.0 + 0.134145 * a * a)
    return (value, slope)

def depthwise(padded, kernel, rows, cols):
    total = jnp.zeros((rows, cols, kernel.shape[1]), jnp.float32)
    for i in range(KSIDE):
        for j in range(KSIDE):
            total = total + kernel[i * KSIDE + j] * padded[i:i + rows, j:j + cols]
    return total

def depthwise_back(padded, kernel, rows, cols):
    total = jnp.zeros((rows, cols, kernel.shape[1]), jnp.float32)
    edge = 2 * (KSIDE // 2)
    for i in range(KSIDE):
        for j in range(KSIDE):
            total = total + kernel[i * KSIDE + j] * padded[edge - i:edge - i + rows, edge - j:edge - j + cols]
    return total

def kernel_terms(padded, grad, rows, cols):
    terms = []
    for i in range(KSIDE):
        for j in range(KSIDE):
            terms.append(lax.optimization_barrier(jnp.sum(padded[i:i + rows, j:j + cols] * grad, axis=(0, 1))))
    return jnp.stack(terms)

def pointwise_back(v, g, gain, bias, w_first, b_first, w_second, scale_res):
    rows, cols, chans = v.shape
    flat = v.reshape(rows * cols, chans)
    mean_v = lax.optimization_barrier(jnp.mean(flat, axis=1, keepdims=True))
    centred = flat - mean_v
    rs = lax.rsqrt(lax.optimization_barrier(jnp.mean(centred * centred, axis=1, keepdims=True)) + 1e-06)
    nh = centred * rs
    normed = (nh * gain + bias).astype(jnp.bfloat16)
    pre = jnp.dot(normed, w_first, preferred_element_type=jnp.float32) + b_first
    value, slope = gelu_parts(pre)
    hidden = value.astype(jnp.bfloat16)
    outer = (g.reshape(rows * cols, chans).astype(jnp.float32) * scale_res).astype(jnp.bfloat16)
    dh = lax.dot_general(outer, w_second, (((1,), (1,)), ((), ())), preferred_element_type=jnp.float32)
    da = (dh * slope).astype(jnp.bfloat16)
    dn = lax.dot_general(da, w_first, (((1,), (1,)), ((), ())), preferred_element_type=jnp.float32)
    q = dn * gain
    du = rs * (q - lax.optimization_barrier(jnp.mean(q, axis=1, keepdims=True)) - nh * lax.optimization_barrier(jnp.mean(q * nh, axis=1, keepdims=True)))
    return (du.astype(jnp.bfloat16).reshape(rows, cols, chans), hidden, outer)

def block_step(x, g, kernel, gain, bias, w_first, b_first, w_second, scale_res):
    half = KSIDE // 2
    rows, cols = (x.shape[0], x.shape[1])
    padded = jnp.pad(x.astype(jnp.float32), ((half, half), (half, half), (0, 0)))
    kern = kernel.astype(jnp.float32)
    v = depthwise(padded, kern, rows, cols)
    du, hidden, outer = pointwise_back(v, g, gain, bias, w_first, b_first, w_second, scale_res)
    du_wide = du.astype(jnp.float32)
    du_pad = jnp.pad(du_wide, ((half, half), (half, half), (0, 0)))
    dx = (g.astype(jnp.float32) + depthwise_back(du_pad, kern, rows, cols)).astype(jnp.bfloat16)
    dk = kernel_terms(padded, du_wide, rows, cols)
    wgrad = lax.dot_general(hidden, outer, (((0,), (0,)), ((), ())), preferred_element_type=jnp.float32)
    return (dx, wgrad, dk)

def reference(stash_down, stash_up, grad_down, grad_up, dw_kernel, norm_gain, norm_bias, w_in, b_in, w_out, layer_scale):
    norm = 1.0 / math.sqrt(2.0 * H_ROWS * COLS)

    def params(k):
        return (dw_kernel[k, 0], norm_gain[k, 0], norm_bias[k, 0], w_in[k, 0], b_in[k, 0], w_out[k, 0], layer_scale[k, 0])
    grads_a = [None] * N_SEGMENT
    grads_b = [None] * N_SEGMENT
    wsum = [None] * N_SEGMENT
    ksum = [None] * N_SEGMENT
    g = grad_down
    for k in range(N_SEGMENT - 1, -1, -1):
        dx, wgrad, dk = block_step(stash_down[k], g, *params(k))
        grads_a[k] = dx
        wsum[k] = wgrad
        ksum[k] = dk
        g = dx
    g = grad_up
    for s in range(N_SEGMENT):
        k = N_SEGMENT - 1 - s
        dx, wgrad, dk = block_step(stash_up[s], g, *params(k))
        grads_b[s] = dx
        wsum[k] = wsum[k] + wgrad
        ksum[k] = ksum[k] + dk
        g = dx
    w_grad = jnp.stack(wsum) * norm
    k_grad = jnp.stack(ksum) * norm
    return (jnp.stack(grads_a), jnp.stack(grads_b), w_grad, k_grad)
```

```python
import functools
import math

import jax
import jax.numpy as jnp
from jax import lax
from jax.experimental import pallas as pl
from jax.experimental.pallas import tpu as pltpu
from jax.sharding import PartitionSpec as P

KSIDE = 7


MESH = pl.DeviceIdType.MESH


def turned(q):
    return q + (q // 2) * (1 - 2 * (q % 2))


def chip_at(k):
    q = k // 4
    r = k % 4
    odd = q % 2
    z = r + odd * (3 - 2 * r)
    return z * 4 + turned(q)


def place_of(p):
    z = p // 4
    q = turned(p % 4)
    odd = q % 2
    return q * 4 + z + odd * (3 - 2 * z)


def gather_kernel(
    n, win, wout, win_all, wout_all, own_sem, send_sem, recv_sem, over_send, over_recv
):
    core = lax.axis_index("segment")
    p = lax.axis_index("space")
    k = place_of(p)
    ways = (chip_at((k + 1) % n), chip_at((k + n - 1) % n))
    barrier = pltpu.get_barrier_semaphore()
    for device in ((core, ways[0]), (core, ways[1]), (1 - core, p)):
        pl.semaphore_signal(barrier, inc=1, device_id=device, device_id_type=MESH)
    pl.semaphore_wait(barrier, 3)

    half = n // 2
    steps = [
        (t, b, d) for t in range(half) for b in (1, 0) for d in (0, 1) if t < half - 1 or b != d
    ]

    def carry(mine, mine_all, other_all, mine_slot):
        def hop(t, b, d):
            origin = chip_at((k + (n - t if d == 0 else t)) % n)
            spot = mine_all.at[b, origin]
            return pltpu.make_async_remote_copy(
                src_ref=mine.at[mine_slot(b)] if t == 0 else spot,
                dst_ref=spot,
                send_sem=send_sem.at[t, b, d],
                recv_sem=recv_sem.at[t, b, d],
                device_id=(core, ways[d]),
                device_id_type=MESH,
            )

        def arrival(t, b, d):
            origin = chip_at((k + (n - t - 1 if d == 0 else t + 1)) % n)
            return mine_all.at[b, origin], other_all.at[b, origin]

        def across(t, b, d):
            spot, _ = arrival(t, b, d)
            return pltpu.make_async_remote_copy(
                src_ref=spot,
                dst_ref=spot,
                send_sem=over_send.at[t, b, d],
                recv_sem=over_recv.at[t, b, d],
                device_id=(1 - core, p),
                device_id_type=MESH,
            )

        for b in (1, 0):
            for d in (0, 1):
                hop(0, b, d).start()
        for t, b, d in steps:
            spot, _ = arrival(t, b, d)
            pltpu.make_async_copy(spot, spot, recv_sem.at[t, b, d]).wait()
            if (t + 1, b, d) in steps:
                hop(t + 1, b, d).start()
            across(t, b, d).start()
        for t, b, d in steps:
            hop(t, b, d).wait_send()
            across(t, b, d).wait_send()
            _, other = arrival(t, b, d)
            pltpu.make_async_copy(other, other, over_recv.at[t, b, d]).wait()

    def own(slot):
        copies = []
        for b in (0, 1):
            copies.append(pltpu.make_async_copy(win.at[slot(b)], win_all.at[b, p], own_sem.at[0, b]))
            copies.append(
                pltpu.make_async_copy(wout.at[slot(b)], wout_all.at[b, p], own_sem.at[1, b])
            )
        return copies

    @pl.when(core == 0)
    def _():
        for c in own(lambda b: b):
            c.start()
        carry(win, win_all, wout_all, lambda b: b)
        for c in own(lambda b: b):
            c.wait()

    @pl.when(core == 1)
    def _():
        for c in own(lambda b: 1 - b):
            c.start()
        carry(wout, wout_all, win_all, lambda b: 1 - b)
        for c in own(lambda b: 1 - b):
            c.wait()


def gathered(w_in, w_out):
    n = lax.axis_size("space")
    win, wout = w_in[0], w_out[0]
    sems = pltpu.SemaphoreType.DMA((n // 2, 2, 2))
    win_all, wout_all = pl.pallas_call(
        functools.partial(gather_kernel, n),
        out_shape=(
            jax.ShapeDtypeStruct((2, n) + win.shape[1:], win.dtype),
            jax.ShapeDtypeStruct((2, n) + wout.shape[1:], wout.dtype),
        ),
        in_specs=[pl.BlockSpec(memory_space=pl.ANY)] * 2,
        out_specs=(pl.BlockSpec(memory_space=pl.ANY),) * 2,
        scratch_shapes=[pltpu.SemaphoreType.DMA((2, 2)), sems, sems, sems, sems],
        compiler_params=pltpu.CompilerParams(collective_id=0, has_side_effects=True),
        name="gather_weights",
    )(win, wout)
    return (
        win_all.reshape(2, n * win.shape[1], win.shape[2]),
        wout_all.reshape(2, n * wout.shape[1], wout.shape[2]),
    )


def sum_kernel(
    part,
    dk,
    out,
    dk_out,
    sa1,
    sb1,
    ra1,
    rb1,
    sa2,
    sb2,
    ra2,
    rb2,
    s3,
    r3,
    kr1,
    ks2,
    kr2,
    ks3,
    kr3,
    send_sem,
    recv_sem,
):
    core = lax.axis_index("segment")
    p = lax.axis_index("space")
    z = p // 4
    y = (p // 2) % 2
    x = p % 2
    half = out.shape[0] // 2
    over_x = (core, z * 4 + y * 2 + 1 - x)
    over_y = (core, z * 4 + (1 - y) * 2 + x)
    over_z = [(core, ((z + j) % 4) * 4 + y * 2 + x) for j in (1, 2, 3)]
    barrier = pltpu.get_barrier_semaphore()
    for device in [over_x, over_y] + over_z:
        pl.semaphore_signal(barrier, inc=1, device_id=device, device_id_type=MESH)

    def sent(src, dst, number, device):
        return pltpu.make_async_remote_copy(
            src_ref=src,
            dst_ref=dst,
            send_sem=send_sem.at[number],
            recv_sem=recv_sem.at[number],
            device_id=device,
            device_id_type=MESH,
        )

    low, high = pl.ds(0, half), pl.ds(half, half)
    for zz in range(4):
        for o in range(2):
            sa1[zz, o] = part[zz, o, 1 - x, low].astype(sa1.dtype)
            sb1[zz, o] = part[zz, 1 - y, o, high].astype(sb1.dtype)
    pl.semaphore_wait(barrier, 5)
    first = [sent(sa1, ra1, 0, over_x), sent(sb1, rb1, 1, over_y), sent(dk, kr1, 2, over_x)]
    for c in first:
        c.start()
    for c in first:
        c.wait_recv()
    for zz in range(4):
        sa2[zz] = (part[zz, 1 - y, x, low] + ra1[zz, 1 - y].astype(jnp.float32)).astype(sa2.dtype)
        sb2[zz] = (part[zz, y, 1 - x, high] + rb1[zz, 1 - x].astype(jnp.float32)).astype(sb2.dtype)
    ks2[...] = dk[...] + kr1[...]
    second = [sent(sa2, ra2, 3, over_y), sent(sb2, rb2, 4, over_x), sent(ks2, kr2, 5, over_y)]
    for c in second:
        c.start()

    def kept(zz):
        a = part[zz, y, x, low] + ra1[zz, y].astype(jnp.float32)
        b = part[zz, y, x, high] + rb1[zz, x].astype(jnp.float32)
        return a, b

    for c in second:
        c.wait_recv()
    ksum = ks2[...] + kr2[...]
    ks3[...] = ksum.astype(ks3.dtype)
    third = []
    for j in (1, 2, 3):
        zz = (z + j) % 4
        a, b = kept(zz)
        s3[j - 1, low] = (a + ra2[zz].astype(jnp.float32)).astype(s3.dtype)
        s3[j - 1, high] = (b + rb2[zz].astype(jnp.float32)).astype(s3.dtype)
        third.append(sent(s3.at[j - 1], r3.at[j - 1], 6 + j, over_z[j - 1]))
        third.append(sent(ks3, kr3.at[j - 1], 9 + j, over_z[j - 1]))
        third[-2].start()
        third[-1].start()
    a, b = kept(z)
    a = a + ra2[z].astype(jnp.float32)
    b = b + rb2[z].astype(jnp.float32)
    for c in third:
        c.wait_recv()
    for j in range(3):
        a = a + r3[j, low].astype(jnp.float32)
        b = b + r3[j, high].astype(jnp.float32)
        ksum = ksum + kr3[j].astype(jnp.float32)
    out[low] = a
    out[high] = b
    dk_out[...] = ksum
    for c in first + second + third:
        c.wait_send()


def summed(part, dk):
    n = lax.axis_size("space")
    share, chans = part.shape[0] // n, part.shape[1]
    part = part.reshape(4, 2, 2, share, chans)
    taps = dk.shape[0]
    dk = jnp.pad(dk, ((0, -taps % 16), (0, 0)))
    half = share // 2
    sent = jnp.bfloat16
    wide = pltpu.VMEM((4, 2, half, chans), sent)
    narrow = pltpu.VMEM((4, half, chans), sent)
    out, dk = pl.pallas_call(
        sum_kernel,
        out_shape=(
            jax.ShapeDtypeStruct((share, chans), jnp.float32),
            jax.ShapeDtypeStruct(dk.shape, jnp.float32),
        ),
        in_specs=[pl.BlockSpec(memory_space=pltpu.VMEM)] * 2,
        out_specs=(pl.BlockSpec(memory_space=pltpu.VMEM),) * 2,
        scratch_shapes=[
            wide,
            wide,
            wide,
            wide,
            narrow,
            narrow,
            narrow,
            narrow,
            pltpu.VMEM((3, share, chans), sent),
            pltpu.VMEM((3, share, chans), sent),
            pltpu.VMEM(dk.shape, jnp.float32),
            pltpu.VMEM(dk.shape, jnp.float32),
            pltpu.VMEM(dk.shape, jnp.float32),
            pltpu.VMEM(dk.shape, sent),
            pltpu.VMEM((3,) + dk.shape, sent),
            pltpu.SemaphoreType.DMA((13,)),
            pltpu.SemaphoreType.DMA((13,)),
        ],
        compiler_params=pltpu.CompilerParams(
            collective_id=1, has_side_effects=True, vmem_limit_bytes=24 * 1024 * 1024
        ),
        name="sum_gradients",
    )(part, dk)
    return out, dk[:taps]


def padded_2(cells, sides, width):
    for axis, dim in sides:
        count = lax.axis_size(axis)
        ends = count - 1
        head = lax.slice_in_dim(cells, 0, width, axis=dim)
        tail = lax.slice_in_dim(cells, cells.shape[dim] - width, cells.shape[dim], axis=dim)
        cells = jnp.concatenate(
            [
                lax.ppermute(tail, axis, [(i, (i + 1) % count) for i in range(ends)]),
                cells,
                lax.ppermute(head, axis, [((i + 1) % count, i) for i in range(ends)]),
            ],
            axis=dim,
        )
    return cells


def passed_along(shard, axis, by):
    devices = lax.axis_size(axis)
    pairs = [(i, i + by) for i in range(devices) if 0 <= i + by < devices]
    return lax.ppermute(shard, axis, pairs)


def as_sent(shard):
    return jax.tree.map(lambda a: a.astype(jnp.bfloat16) if a.dtype == jnp.float32 else a, shard)


def swapped(block, axis, stride):
    count = lax.axis_size(axis)
    route = []
    for low in range(count):
        high = low | 1 << stride
        if high != low and high < count:
            route += [(low, high), (high, low)]
    return lax.ppermute(block, axis, route)


def gelu_parts(a):
    inner = 0.7978845608 * (a + 0.044715 * a * a * a)
    th = jnp.tanh(inner)
    value = 0.5 * a * (1.0 + th)
    slope = 0.5 * (1.0 + th) + 0.5 * a * (1.0 - th * th) * 0.7978845608 * (1.0 + 0.134145 * a * a)
    return (value, slope)


def grouped_conv(padded, filters):
    chans = padded.shape[2]
    result = lax.conv_general_dilated(
        padded[None],
        filters,
        (1, 1),
        "VALID",
        dimension_numbers=("NHWC", "HWIO", "NHWC"),
        feature_group_count=chans,
        precision=lax.Precision.HIGHEST,
    )
    return result[0]


def depthwise(padded, kernel):
    chans = kernel.shape[1]
    filters = kernel.reshape(KSIDE, KSIDE, 1, chans)
    return grouped_conv(padded, filters)


def depthwise_back(padded, kernel):
    chans = kernel.shape[1]
    filters = kernel.reshape(KSIDE, KSIDE, 1, chans)[::-1, ::-1]
    return grouped_conv(padded, filters)


def kernel_terms(padded, grad):
    rows, cols, chans = grad.shape
    filters = grad.reshape(rows, cols, 1, chans)
    return grouped_conv(padded, filters).reshape(KSIDE * KSIDE, chans)


def pointwise_back(v, g, gain, bias, w_first, b_first, w_second, scale_res):
    rows, cols, chans = v.shape
    flat = v.reshape(rows * cols, chans)
    mean_v = jnp.mean(flat, axis=1, keepdims=True)
    centred = flat - mean_v
    rs = lax.rsqrt(jnp.mean(centred * centred, axis=1, keepdims=True) + 1e-06)
    nh = centred * rs
    normed = (nh * gain + bias).astype(jnp.bfloat16)
    pre = jnp.dot(normed, w_first, preferred_element_type=jnp.float32) + b_first
    value, slope = gelu_parts(pre)
    hidden = value.astype(jnp.bfloat16)
    outer = (g.reshape(rows * cols, chans).astype(jnp.float32) * scale_res).astype(jnp.bfloat16)
    dh = lax.dot_general(
        outer, w_second, (((1,), (1,)), ((), ())), preferred_element_type=jnp.float32
    )
    da = (dh * slope).astype(jnp.bfloat16)
    dn = lax.dot_general(da, w_first, (((1,), (1,)), ((), ())), preferred_element_type=jnp.float32)
    q = dn * gain
    du = rs * (
        q - jnp.mean(q, axis=1, keepdims=True) - nh * jnp.mean(q * nh, axis=1, keepdims=True)
    )
    return (du.astype(jnp.bfloat16).reshape(rows, cols, chans), hidden, outer)


def per_device(
    stash_down,
    stash_up,
    grad_down,
    grad_up,
    dw_kernel,
    norm_gain,
    norm_bias,
    w_in,
    b_in,
    w_out,
    layer_scale,
):
    segments = lax.axis_size("segment")
    me = lax.axis_index("segment")
    half = KSIDE // 2
    rows, cols, chans = (stash_down.shape[1], stash_down.shape[2], stash_down.shape[3])
    hidden_units = w_in.shape[3]
    norm = 1.0 / math.sqrt(2.0 * rows * lax.axis_size("space") * cols)
    paired = segments == 2 and lax.axis_size("space") == 16
    if paired:
        w_in_all, w_out_all = gathered(w_in, w_out)
    else:
        w_in_all, w_out_all = (
            lax.all_gather(w_in, "space", axis=2, tiled=True)[0],
            lax.all_gather(w_out, "space", axis=2, tiled=True)[0],
        )
    x_down = stash_down[0]
    x_up = stash_up[0]
    rimmed_both = padded_2(jnp.stack([x_down, x_up]), (("space", 1),), half)
    down_in = grad_down
    up_in = grad_up
    out_down = jnp.zeros_like(grad_down)
    out_up = jnp.zeros_like(grad_up)
    tokens = rows * cols
    hid_down = jnp.zeros((tokens, hidden_units), jnp.bfloat16)
    hid_up = jnp.zeros((tokens, hidden_units), jnp.bfloat16)
    outer_down = jnp.zeros((tokens, chans), jnp.bfloat16)
    outer_up = jnp.zeros((tokens, chans), jnp.bfloat16)
    kern_down = jnp.zeros((KSIDE * KSIDE, chans), jnp.float32)
    kern_up = jnp.zeros((KSIDE * KSIDE, chans), jnp.float32)
    for step in range(segments):
        on_up = me == step
        on_down = me == segments - 1 - step
        active = jnp.logical_or(on_up, on_down)
        pick = on_up.astype(jnp.int32)

        def select(array):
            return lax.dynamic_index_in_dim(array[0], pick, 0, keepdims=False)

        rimmed = jnp.where(on_up, rimmed_both[1], rimmed_both[0])
        padded = jnp.pad(rimmed.astype(jnp.float32), ((0, 0), (half, half), (0, 0)))
        g = jnp.where(on_up, up_in, down_in)
        kern = select(dw_kernel).astype(jnp.float32)

        def chosen(array):
            if paired:
                return array[segments - 1 - step]
            return lax.dynamic_index_in_dim(array, pick, 0, keepdims=False)

        def front_live():
            v = depthwise(padded, kern)
            return pointwise_back(
                v,
                g,
                select(norm_gain),
                select(norm_bias),
                chosen(w_in_all),
                select(b_in),
                chosen(w_out_all),
                select(layer_scale),
            )

        def front_spare():
            return (
                jnp.zeros((rows, cols, chans), jnp.bfloat16),
                jnp.zeros((tokens, hidden_units), jnp.bfloat16),
                jnp.zeros((tokens, chans), jnp.bfloat16),
            )

        du, hidden, outer = front_live() if paired else lax.cond(active, front_live, front_spare)
        du_rimmed = padded_2(du, (("space", 0),), half)

        def back_live():
            du_pad = jnp.pad(du_rimmed.astype(jnp.float32), ((0, 0), (half, half), (0, 0)))
            dx_new = (g.astype(jnp.float32) + depthwise_back(du_pad, kern)).astype(jnp.bfloat16)
            dk_new = kernel_terms(padded, du.astype(jnp.float32))
            return (dx_new, dk_new)

        def back_spare():
            return (
                jnp.zeros((rows, cols, chans), jnp.bfloat16),
                jnp.zeros((KSIDE * KSIDE, chans), jnp.float32),
            )

        dx, dk = back_live() if paired else lax.cond(active, back_live, back_spare)
        out_down = jnp.where(on_down, dx, out_down)
        out_up = jnp.where(on_up, dx, out_up)
        kern_down = jnp.where(on_down, dk, kern_down)
        kern_up = jnp.where(on_up, dk, kern_up)
        hid_down = jnp.where(on_down, hidden, hid_down)
        hid_up = jnp.where(on_up, hidden, hid_up)
        outer_down = jnp.where(on_down, outer, outer_down)
        outer_up = jnp.where(on_up, outer, outer_up)
        if step + 1 < segments:
            down_in = passed_along(dx, "segment", -1)
            up_in = passed_along(dx, "segment", 1)
    levels = segments.bit_length() - 1
    for bit in range(levels):
        kern_up = swapped(as_sent(kern_up), "segment", bit).astype(kern_up.dtype)
    share = w_out.shape[2]
    joined = jnp.concatenate([hid_up, outer_up], axis=1)
    for bit in range(levels):
        joined = swapped(joined, "segment", bit)
    all_hidden = jnp.concatenate([hid_down, joined[:, :hidden_units]], axis=0)
    all_outer = jnp.concatenate([outer_down, joined[:, hidden_units:]], axis=0)
    columns = lax.slice_in_dim(all_hidden, 0, share * lax.axis_size("space"), axis=1)
    w_part = (
        lax.dot_general(
            columns, all_outer, (((0,), (0,)), ((), ())), preferred_element_type=jnp.float32
        )
        * norm
    )
    k_part = (kern_down + kern_up) * norm
    if paired:
        w_grad, k_grad = summed(w_part, k_part)
    else:
        w_grad = lax.psum_scatter(w_part, "space", scatter_dimension=0, tiled=True)
        k_grad = lax.psum(k_part, "space")
    return (out_down[None], out_up[None], w_grad[None], k_grad[None])


def solution(mesh):
    return jax.shard_map(
        per_device,
        mesh=mesh,
        in_specs=(
            P("segment", "space", None, None),
            P("segment", "space", None, None),
            P("space", None, None),
            P("space", None, None),
            P("segment", None, None, None),
            P("segment", None, None),
            P("segment", None, None),
            P("segment", None, "space", None),
            P("segment", None, None),
            P("segment", None, "space", None),
            P("segment", None, None),
        ),
        out_specs=(
            P("segment", "space", None, None),
            P("segment", "space", None, None),
            P("segment", "space", None),
            P("segment", None, None),
        ),
        check_vma=False,
    )
```

```python
import functools
import math

import jax
import jax.numpy as jnp
from jax import lax
from jax.experimental import pallas as pl
from jax.experimental.pallas import tpu as pltpu
from jax.sharding import PartitionSpec as P

KSIDE = 7


MESH = pl.DeviceIdType.MESH


def gather_kernel(
    win,
    wout,
    x,
    win_all,
    wout_all,
    above,
    below,
    own_sem,
    z_send,
    z_recv,
    one_send,
    one_recv,
    two_send,
    two_recv,
    over_send,
    over_recv,
    rim_send,
    rim_recv,
):
    core = lax.axis_index("segment")
    p = lax.axis_index("space")
    z = p // 4
    y = (p // 2) % 2
    xx = p % 2
    after, before = (core, (p + 1) % 16), (core, (p + 15) % 16)
    over_x = (core, z * 4 + y * 2 + 1 - xx)
    over_y = (core, z * 4 + (1 - y) * 2 + xx)
    over_z = {j: (core, ((z + j) % 4) * 4 + y * 2 + xx) for j in (1, 2, 3)}
    other_core = (1 - core, p)
    barrier = pltpu.get_barrier_semaphore()
    greeted = [over_x, over_y, other_core, after, before] + list(over_z.values())
    for device in greeted:
        pl.semaphore_signal(barrier, inc=1, device_id=device, device_id_type=MESH)
    pl.semaphore_wait(barrier, len(greeted))

    def remote(src, dst, send, recv, device):
        return pltpu.make_async_remote_copy(
            src_ref=src,
            dst_ref=dst,
            send_sem=send,
            recv_sem=recv,
            device_id=device,
            device_id_type=MESH,
        )

    width, rows = above.shape[1], x.shape[1]
    rims = []
    for m in (0, 1):
        rims.append(
            remote(
                x.at[m, pl.ds(rows - width, width)],
                above.at[m],
                rim_send.at[m, 0],
                rim_recv.at[m, 0],
                after,
            )
        )
        rims.append(
            remote(
                x.at[m, pl.ds(0, width)], below.at[m], rim_send.at[m, 1], rim_recv.at[m, 1], before
            )
        )

    def carry(mine, mine_all, other_all, slot):
        def cell(j, turned_y, turned_x):
            yy = 1 - y if turned_y else y
            xo = 1 - xx if turned_x else xx
            return ((z + 4 - j) % 4) * 4 + yy * 2 + xo

        def first(b):
            return (over_x, 0, 1) if b == 1 else (over_y, 1, 0)

        def second(b):
            return (over_y, 1, 0) if b == 1 else (over_x, 0, 1)

        pending = []

        def start(copy):
            copy.start()
            pending.append(copy)

        arrivals = []

        def across(origin, b, number):
            start(
                remote(
                    mine_all.at[b, origin],
                    mine_all.at[b, origin],
                    over_send.at[number, b],
                    over_recv.at[number, b],
                    other_core,
                )
            )
            arrivals.append((other_all.at[b, origin], over_recv.at[number, b]))

        def landed(ref, sem):
            pltpu.make_async_copy(ref, ref, sem).wait()

        def line(j, b):
            origin = cell(j, 0, 0)
            spot = mine_all.at[b, origin]
            if j:
                landed(spot, z_recv.at[j, b])
            src = spot if j else mine.at[slot(b)]
            start(remote(src, spot, one_send.at[j, b], one_recv.at[j, b], first(b)[0]))
            start(remote(src, spot, two_send.at[j, b, 0], two_recv.at[j, b, 0], second(b)[0]))
            if j:
                across(origin, b, j)

        def once(j, b):
            _, ty, tx = first(b)
            origin = cell(j, ty, tx)
            spot = mine_all.at[b, origin]
            landed(spot, one_recv.at[j, b])
            start(remote(spot, spot, two_send.at[j, b, 1], two_recv.at[j, b, 1], second(b)[0]))
            across(origin, b, 4 + j)

        def twice(j, b):
            _, ty, tx = second(b)
            for which, origin in enumerate((cell(j, ty, tx), cell(j, 1, 1))):
                landed(mine_all.at[b, origin], two_recv.at[j, b, which])
                across(origin, b, 8 + 2 * j + which)

        for b in (1, 0):
            line(0, b)
        for j in (1, 3, 2):
            for b in (1, 0):
                spot = mine_all.at[b, p]
                start(remote(mine.at[slot(b)], spot, z_send.at[j, b], z_recv.at[j, b], over_z[j]))
        for c in rims:
            c.start()
        for act, j in (
            (once, 0),
            (line, 1),
            (line, 3),
            (once, 1),
            (twice, 0),
            (line, 2),
            (once, 3),
            (twice, 1),
            (once, 2),
            (twice, 3),
            (twice, 2),
        ):
            for b in (1, 0):
                act(j, b)
        for c in rims:
            c.wait()
        for ref, sem in arrivals:
            landed(ref, sem)
        for c in pending:
            c.wait_send()

    def own(slot):
        copies = []
        for b in (0, 1):
            copies.append(pltpu.make_async_copy(win.at[slot(b)], win_all.at[b, p], own_sem.at[0, b]))
            copies.append(
                pltpu.make_async_copy(wout.at[slot(b)], wout_all.at[b, p], own_sem.at[1, b])
            )
        return copies

    @pl.when(core == 0)
    def _():
        for c in own(lambda b: b):
            c.start()
        carry(win, win_all, wout_all, lambda b: b)
        for c in own(lambda b: b):
            c.wait()

    @pl.when(core == 1)
    def _():
        for c in own(lambda b: 1 - b):
            c.start()
        carry(wout, wout_all, win_all, lambda b: 1 - b)
        for c in own(lambda b: 1 - b):
            c.wait()


def gathered(w_in, w_out, x, width):
    n = lax.axis_size("space")
    p = lax.axis_index("space")
    win, wout = w_in[0], w_out[0]
    dma = pltpu.SemaphoreType.DMA
    rim = jax.ShapeDtypeStruct((2, width) + x.shape[2:], x.dtype)
    win_all, wout_all, above, below = pl.pallas_call(
        gather_kernel,
        out_shape=(
            jax.ShapeDtypeStruct((2, n) + win.shape[1:], win.dtype),
            jax.ShapeDtypeStruct((2, n) + wout.shape[1:], wout.dtype),
            rim,
            rim,
        ),
        in_specs=[pl.BlockSpec(memory_space=pl.ANY)] * 3,
        out_specs=(pl.BlockSpec(memory_space=pl.ANY),) * 4,
        scratch_shapes=[
            dma((2, 2)),
            dma((4, 2)),
            dma((4, 2)),
            dma((4, 2)),
            dma((4, 2)),
            dma((4, 2, 2)),
            dma((4, 2, 2)),
            dma((16, 2)),
            dma((16, 2)),
            dma((2, 2)),
            dma((2, 2)),
        ],
        compiler_params=pltpu.CompilerParams(collective_id=0, has_side_effects=True),
        name="gather_weights",
    )(win, wout, x)
    above = jnp.where(p == 0, jnp.zeros_like(above), above)
    below = jnp.where(p == n - 1, jnp.zeros_like(below), below)
    return (
        win_all.reshape(2, n * win.shape[1], win.shape[2]),
        wout_all.reshape(2, n * wout.shape[1], wout.shape[2]),
        jnp.concatenate([above, x, below], axis=1),
    )


def rim_kernel(n, du, out, send_sem, recv_sem):
    core = lax.axis_index("segment")
    p = lax.axis_index("space")
    after, before = (core, (p + 1) % n), (core, (p + n - 1) % n)
    rows = du.shape[0]
    width = (out.shape[0] - rows) // 2
    barrier = pltpu.get_barrier_semaphore()
    for device in (after, before):
        pl.semaphore_signal(barrier, inc=1, device_id=device, device_id_type=MESH)
    pl.semaphore_wait(barrier, 2)
    top, bottom = pl.ds(0, width), pl.ds(width + rows, width)
    down = pltpu.make_async_remote_copy(
        src_ref=du.at[pl.ds(rows - width, width)],
        dst_ref=out.at[top],
        send_sem=send_sem.at[0],
        recv_sem=recv_sem.at[0],
        device_id=after,
        device_id_type=MESH,
    )
    up = pltpu.make_async_remote_copy(
        src_ref=du.at[top],
        dst_ref=out.at[bottom],
        send_sem=send_sem.at[1],
        recv_sem=recv_sem.at[1],
        device_id=before,
        device_id_type=MESH,
    )
    down.start()
    up.start()
    out[pl.ds(width, rows)] = du[...]
    down.wait()
    up.wait()

    @pl.when(p == 0)
    def _():
        out[top] = jnp.zeros((width,) + du.shape[1:], out.dtype)

    @pl.when(p == n - 1)
    def _():
        out[bottom] = jnp.zeros((width,) + du.shape[1:], out.dtype)


def rimmed_by_kernel(du, width):
    n = lax.axis_size("space")
    return pl.pallas_call(
        functools.partial(rim_kernel, n),
        out_shape=jax.ShapeDtypeStruct((du.shape[0] + 2 * width,) + du.shape[1:], du.dtype),
        in_specs=[pl.BlockSpec(memory_space=pltpu.VMEM)],
        out_specs=pl.BlockSpec(memory_space=pltpu.VMEM),
        scratch_shapes=[pltpu.SemaphoreType.DMA((2,)), pltpu.SemaphoreType.DMA((2,))],
        compiler_params=pltpu.CompilerParams(collective_id=2, has_side_effects=True),
        name="gradient_rims",
    )(du)


def sum_kernel(
    part,
    dk,
    out,
    dk_out,
    sa1,
    sb1,
    ra1,
    rb1,
    sa2,
    sb2,
    ra2,
    rb2,
    s3,
    r3,
    kr1,
    ks2,
    kr2,
    ks3,
    kr3,
    send_sem,
    recv_sem,
):
    core = lax.axis_index("segment")
    p = lax.axis_index("space")
    z = p // 4
    y = (p // 2) % 2
    x = p % 2
    half = out.shape[0] // 2
    over_x = (core, z * 4 + y * 2 + 1 - x)
    over_y = (core, z * 4 + (1 - y) * 2 + x)
    over_z = [(core, ((z + j) % 4) * 4 + y * 2 + x) for j in (1, 2, 3)]
    barrier = pltpu.get_barrier_semaphore()
    for device in [over_x, over_y] + over_z:
        pl.semaphore_signal(barrier, inc=1, device_id=device, device_id_type=MESH)

    def sent(src, dst, number, device):
        return pltpu.make_async_remote_copy(
            src_ref=src,
            dst_ref=dst,
            send_sem=send_sem.at[number],
            recv_sem=recv_sem.at[number],
            device_id=device,
            device_id_type=MESH,
        )

    low, high = pl.ds(0, half), pl.ds(half, half)
    for zz in range(4):
        for o in range(2):
            sa1[zz, o] = part[zz, o, 1 - x, low].astype(sa1.dtype)
            sb1[zz, o] = part[zz, 1 - y, o, high].astype(sb1.dtype)
    pl.semaphore_wait(barrier, 5)
    first = [sent(sa1, ra1, 0, over_x), sent(sb1, rb1, 1, over_y), sent(dk, kr1, 2, over_x)]
    for c in first:
        c.start()
    for c in first:
        c.wait_recv()
    for zz in range(4):
        sa2[zz] = (part[zz, 1 - y, x, low] + ra1[zz, 1 - y].astype(jnp.float32)).astype(sa2.dtype)
        sb2[zz] = (part[zz, y, 1 - x, high] + rb1[zz, 1 - x].astype(jnp.float32)).astype(sb2.dtype)
    ks2[...] = dk[...] + kr1[...]
    second = [sent(sa2, ra2, 3, over_y), sent(sb2, rb2, 4, over_x), sent(ks2, kr2, 5, over_y)]
    for c in second:
        c.start()

    def kept(zz):
        a = part[zz, y, x, low] + ra1[zz, y].astype(jnp.float32)
        b = part[zz, y, x, high] + rb1[zz, x].astype(jnp.float32)
        return a, b

    for c in second:
        c.wait_recv()
    ksum = ks2[...] + kr2[...]
    ks3[...] = ksum.astype(ks3.dtype)
    third = []
    for j in (1, 2, 3):
        zz = (z + j) % 4
        a, b = kept(zz)
        s3[j - 1, low] = (a + ra2[zz].astype(jnp.float32)).astype(s3.dtype)
        s3[j - 1, high] = (b + rb2[zz].astype(jnp.float32)).astype(s3.dtype)
        third.append(sent(s3.at[j - 1], r3.at[j - 1], 6 + j, over_z[j - 1]))
        third.append(sent(ks3, kr3.at[j - 1], 9 + j, over_z[j - 1]))
        third[-2].start()
        third[-1].start()
    a, b = kept(z)
    a = a + ra2[z].astype(jnp.float32)
    b = b + rb2[z].astype(jnp.float32)
    for c in third:
        c.wait_recv()
    for j in range(3):
        a = a + r3[j, low].astype(jnp.float32)
        b = b + r3[j, high].astype(jnp.float32)
        ksum = ksum + kr3[j].astype(jnp.float32)
    out[low] = a
    out[high] = b
    dk_out[...] = ksum
    for c in first + second + third:
        c.wait_send()


def summed(part, dk):
    n = lax.axis_size("space")
    share, chans = part.shape[0] // n, part.shape[1]
    part = part.reshape(4, 2, 2, share, chans)
    taps = dk.shape[0]
    dk = jnp.pad(dk, ((0, -taps % 16), (0, 0)))
    half = share // 2
    sent = jnp.bfloat16
    wide = pltpu.VMEM((4, 2, half, chans), sent)
    narrow = pltpu.VMEM((4, half, chans), sent)
    out, dk = pl.pallas_call(
        sum_kernel,
        out_shape=(
            jax.ShapeDtypeStruct((share, chans), jnp.float32),
            jax.ShapeDtypeStruct(dk.shape, jnp.float32),
        ),
        in_specs=[pl.BlockSpec(memory_space=pltpu.VMEM)] * 2,
        out_specs=(pl.BlockSpec(memory_space=pltpu.VMEM),) * 2,
        scratch_shapes=[
            wide,
            wide,
            wide,
            wide,
            narrow,
            narrow,
            narrow,
            narrow,
            pltpu.VMEM((3, share, chans), sent),
            pltpu.VMEM((3, share, chans), sent),
            pltpu.VMEM(dk.shape, jnp.float32),
            pltpu.VMEM(dk.shape, jnp.float32),
            pltpu.VMEM(dk.shape, jnp.float32),
            pltpu.VMEM(dk.shape, sent),
            pltpu.VMEM((3,) + dk.shape, sent),
            pltpu.SemaphoreType.DMA((13,)),
            pltpu.SemaphoreType.DMA((13,)),
        ],
        compiler_params=pltpu.CompilerParams(
            collective_id=1, has_side_effects=True, vmem_limit_bytes=24 * 1024 * 1024
        ),
        name="sum_gradients",
    )(part, dk)
    return out, dk[:taps]


def padded_2(cells, sides, width):
    for axis, dim in sides:
        count = lax.axis_size(axis)
        ends = count - 1
        head = lax.slice_in_dim(cells, 0, width, axis=dim)
        tail = lax.slice_in_dim(cells, cells.shape[dim] - width, cells.shape[dim], axis=dim)
        cells = jnp.concatenate(
            [
                lax.ppermute(tail, axis, [(i, (i + 1) % count) for i in range(ends)]),
                cells,
                lax.ppermute(head, axis, [((i + 1) % count, i) for i in range(ends)]),
            ],
            axis=dim,
        )
    return cells


def passed_along(shard, axis, by):
    devices = lax.axis_size(axis)
    pairs = [(i, i + by) for i in range(devices) if 0 <= i + by < devices]
    return lax.ppermute(shard, axis, pairs)


def as_sent(shard):
    return jax.tree.map(lambda a: a.astype(jnp.bfloat16) if a.dtype == jnp.float32 else a, shard)


def swapped(block, axis, stride):
    count = lax.axis_size(axis)
    route = []
    for low in range(count):
        high = low | 1 << stride
        if high != low and high < count:
            route += [(low, high), (high, low)]
    return lax.ppermute(block, axis, route)


def gelu_parts(a):
    inner = 0.7978845608 * (a + 0.044715 * a * a * a)
    th = jnp.tanh(inner)
    value = 0.5 * a * (1.0 + th)
    slope = 0.5 * (1.0 + th) + 0.5 * a * (1.0 - th * th) * 0.7978845608 * (1.0 + 0.134145 * a * a)
    return (value, slope)


def grouped_conv(padded, filters):
    chans = padded.shape[2]
    result = lax.conv_general_dilated(
        padded[None],
        filters,
        (1, 1),
        "VALID",
        dimension_numbers=("NHWC", "HWIO", "NHWC"),
        feature_group_count=chans,
        precision=lax.Precision.HIGHEST,
    )
    return result[0]


def depthwise(padded, kernel):
    chans = kernel.shape[1]
    filters = kernel.reshape(KSIDE, KSIDE, 1, chans)
    return grouped_conv(padded, filters)


def depthwise_back(padded, kernel):
    chans = kernel.shape[1]
    filters = kernel.reshape(KSIDE, KSIDE, 1, chans)[::-1, ::-1]
    return grouped_conv(padded, filters)


def kernel_terms(padded, grad):
    rows, cols, chans = grad.shape
    filters = grad.reshape(rows, cols, 1, chans)
    return grouped_conv(padded, filters).reshape(KSIDE * KSIDE, chans)


def pointwise_back(v, g, gain, bias, w_first, b_first, w_second, scale_res):
    rows, cols, chans = v.shape
    flat = v.reshape(rows * cols, chans)
    mean_v = jnp.mean(flat, axis=1, keepdims=True)
    centred = flat - mean_v
    rs = lax.rsqrt(jnp.mean(centred * centred, axis=1, keepdims=True) + 1e-06)
    nh = centred * rs
    normed = (nh * gain + bias).astype(jnp.bfloat16)
    pre = jnp.dot(normed, w_first, preferred_element_type=jnp.float32) + b_first
    value, slope = gelu_parts(pre)
    hidden = value.astype(jnp.bfloat16)
    outer = (g.reshape(rows * cols, chans).astype(jnp.float32) * scale_res).astype(jnp.bfloat16)
    dh = lax.dot_general(
        outer, w_second, (((1,), (1,)), ((), ())), preferred_element_type=jnp.float32
    )
    da = (dh * slope).astype(jnp.bfloat16)
    dn = lax.dot_general(da, w_first, (((1,), (1,)), ((), ())), preferred_element_type=jnp.float32)
    q = dn * gain
    du = rs * (
        q - jnp.mean(q, axis=1, keepdims=True) - nh * jnp.mean(q * nh, axis=1, keepdims=True)
    )
    return (du.astype(jnp.bfloat16).reshape(rows, cols, chans), hidden, outer)


def per_device(
    stash_down,
    stash_up,
    grad_down,
    grad_up,
    dw_kernel,
    norm_gain,
    norm_bias,
    w_in,
    b_in,
    w_out,
    layer_scale,
):
    segments = lax.axis_size("segment")
    me = lax.axis_index("segment")
    half = KSIDE // 2
    rows, cols, chans = (stash_down.shape[1], stash_down.shape[2], stash_down.shape[3])
    hidden_units = w_in.shape[3]
    norm = 1.0 / math.sqrt(2.0 * rows * lax.axis_size("space") * cols)
    paired = segments == 2 and lax.axis_size("space") == 16
    if paired:
        w_in_all, w_out_all, rimmed_both = gathered(
            w_in, w_out, jnp.concatenate([stash_down, stash_up]), half
        )
    else:
        w_in_all, w_out_all = (
            lax.all_gather(w_in, "space", axis=2, tiled=True)[0],
            lax.all_gather(w_out, "space", axis=2, tiled=True)[0],
        )
        both = jnp.concatenate([stash_down, stash_up])
        rimmed_both = padded_2(both, (("space", 1),), half)
    down_in = grad_down
    up_in = grad_up
    out_down = jnp.zeros_like(grad_down)
    out_up = jnp.zeros_like(grad_up)
    tokens = rows * cols
    hid_down = jnp.zeros((tokens, hidden_units), jnp.bfloat16)
    hid_up = jnp.zeros((tokens, hidden_units), jnp.bfloat16)
    outer_down = jnp.zeros((tokens, chans), jnp.bfloat16)
    outer_up = jnp.zeros((tokens, chans), jnp.bfloat16)
    kern_down = jnp.zeros((KSIDE * KSIDE, chans), jnp.float32)
    kern_up = jnp.zeros((KSIDE * KSIDE, chans), jnp.float32)
    for step in range(segments):
        on_up = me == step
        on_down = me == segments - 1 - step
        active = jnp.logical_or(on_up, on_down)
        pick = on_up.astype(jnp.int32)

        def select(array):
            return lax.dynamic_index_in_dim(array[0], pick, 0, keepdims=False)

        rimmed = jnp.where(on_up, rimmed_both[1], rimmed_both[0])
        padded = jnp.pad(rimmed.astype(jnp.float32), ((0, 0), (half, half), (0, 0)))
        g = jnp.where(on_up, up_in, down_in)
        kern = select(dw_kernel).astype(jnp.float32)

        def chosen(array):
            if paired:
                return array[segments - 1 - step]
            return lax.dynamic_index_in_dim(array, pick, 0, keepdims=False)

        def front_live():
            v = depthwise(padded, kern)
            return pointwise_back(
                v,
                g,
                select(norm_gain),
                select(norm_bias),
                chosen(w_in_all),
                select(b_in),
                chosen(w_out_all),
                select(layer_scale),
            )

        def front_spare():
            return (
                jnp.zeros((rows, cols, chans), jnp.bfloat16),
                jnp.zeros((tokens, hidden_units), jnp.bfloat16),
                jnp.zeros((tokens, chans), jnp.bfloat16),
            )

        du, hidden, outer = front_live() if paired else lax.cond(active, front_live, front_spare)
        if paired:
            du_rimmed = rimmed_by_kernel(du, half)
        else:
            du_rimmed = padded_2(du, (("space", 0),), half)

        def back_live():
            du_pad = jnp.pad(du_rimmed.astype(jnp.float32), ((0, 0), (half, half), (0, 0)))
            dx_new = (g.astype(jnp.float32) + depthwise_back(du_pad, kern)).astype(jnp.bfloat16)
            dk_new = kernel_terms(padded, du.astype(jnp.float32))
            return (dx_new, dk_new)

        def back_spare():
            return (
                jnp.zeros((rows, cols, chans), jnp.bfloat16),
                jnp.zeros((KSIDE * KSIDE, chans), jnp.float32),
            )

        dx, dk = back_live() if paired else lax.cond(active, back_live, back_spare)
        out_down = jnp.where(on_down, dx, out_down)
        out_up = jnp.where(on_up, dx, out_up)
        kern_down = jnp.where(on_down, dk, kern_down)
        kern_up = jnp.where(on_up, dk, kern_up)
        hid_down = jnp.where(on_down, hidden, hid_down)
        hid_up = jnp.where(on_up, hidden, hid_up)
        outer_down = jnp.where(on_down, outer, outer_down)
        outer_up = jnp.where(on_up, outer, outer_up)
        if paired and step == 0:
            down_in = up_in = swapped(dx, "segment", 0)
        elif step + 1 < segments:
            down_in = passed_along(dx, "segment", -1)
            up_in = passed_along(dx, "segment", 1)
    levels = segments.bit_length() - 1
    for bit in range(levels):
        kern_up = swapped(as_sent(kern_up), "segment", bit).astype(kern_up.dtype)
    share = w_out.shape[2]
    joined = jnp.concatenate([hid_up, outer_up], axis=1)
    for bit in range(levels):
        joined = swapped(joined, "segment", bit)
    all_hidden = jnp.concatenate([hid_down, joined[:, :hidden_units]], axis=0)
    all_outer = jnp.concatenate([outer_down, joined[:, hidden_units:]], axis=0)
    columns = lax.slice_in_dim(all_hidden, 0, share * lax.axis_size("space"), axis=1)
    w_part = (
        lax.dot_general(
            columns, all_outer, (((0,), (0,)), ((), ())), preferred_element_type=jnp.float32
        )
        * norm
    )
    k_part = (kern_down + kern_up) * norm
    if paired:
        w_grad, k_grad = summed(w_part, k_part)
    else:
        w_grad = lax.psum_scatter(w_part, "space", scatter_dimension=0, tiled=True)
        k_grad = lax.psum(k_part, "space")
    return (out_down[None], out_up[None], w_grad[None], k_grad[None])


def solution(mesh):
    return jax.shard_map(
        per_device,
        mesh=mesh,
        in_specs=(
            P("segment", "space", None, None),
            P("segment", "space", None, None),
            P("space", None, None),
            P("space", None, None),
            P("segment", None, None, None),
            P("segment", None, None),
            P("segment", None, None),
            P("segment", None, "space", None),
            P("segment", None, None),
            P("segment", None, "space", None),
            P("segment", None, None),
        ),
        out_specs=(
            P("segment", "space", None, None),
            P("segment", "space", None, None),
            P("segment", "space", None),
            P("segment", None, None),
        ),
        check_vma=False,
    )
```

```python
import functools
import math

import jax
import jax.numpy as jnp
from jax import lax
from jax.experimental import pallas as pl
from jax.experimental.pallas import tpu as pltpu
from jax.sharding import PartitionSpec as P

KSIDE = 7


MESH = pl.DeviceIdType.MESH


def gather_kernel(
    win,
    wout,
    x_down,
    x_up,
    win_all,
    wout_all,
    above,
    below,
    own_sem,
    z_send,
    z_recv,
    one_send,
    one_recv,
    two_send,
    two_recv,
    over_send,
    over_recv,
    rim_send,
    rim_recv,
):
    core = lax.axis_index("segment")
    p = lax.axis_index("space")
    z = p // 4
    y = (p // 2) % 2
    xx = p % 2
    after, before = (core, (p + 1) % 16), (core, (p + 15) % 16)
    over_x = (core, z * 4 + y * 2 + 1 - xx)
    over_y = (core, z * 4 + (1 - y) * 2 + xx)
    over_z = {j: (core, ((z + j) % 4) * 4 + y * 2 + xx) for j in (1, 2, 3)}
    other_core = (1 - core, p)
    barrier = pltpu.get_barrier_semaphore()
    greeted = [over_x, over_y, other_core, after, before] + list(over_z.values())
    for device in greeted:
        pl.semaphore_signal(barrier, inc=1, device_id=device, device_id_type=MESH)
    pl.semaphore_wait(barrier, len(greeted))

    def remote(src, dst, send, recv, device):
        return pltpu.make_async_remote_copy(
            src_ref=src,
            dst_ref=dst,
            send_sem=send,
            recv_sem=recv,
            device_id=device,
            device_id_type=MESH,
        )

    width, rows = above.shape[1], x_up.shape[0]
    rims = []
    for m, x in enumerate((x_down, x_up)):
        rims.append(
            remote(
                x.at[pl.ds(rows - width, width)],
                above.at[m],
                rim_send.at[m, 0],
                rim_recv.at[m, 0],
                after,
            )
        )
        rims.append(
            remote(
                x.at[pl.ds(0, width)], below.at[m], rim_send.at[m, 1], rim_recv.at[m, 1], before
            )
        )

    def carry(mine, mine_all, other_all, slot):
        def cell(j, turned_y, turned_x):
            yy = 1 - y if turned_y else y
            xo = 1 - xx if turned_x else xx
            return ((z + 4 - j) % 4) * 4 + yy * 2 + xo

        def first(b):
            return (over_x, 0, 1) if b == 1 else (over_y, 1, 0)

        def second(b):
            return (over_y, 1, 0) if b == 1 else (over_x, 0, 1)

        pending = []

        def start(copy):
            copy.start()
            pending.append(copy)

        arrivals = []

        def across(origin, b, number):
            start(
                remote(
                    mine_all.at[b, origin],
                    mine_all.at[b, origin],
                    over_send.at[number, b],
                    over_recv.at[number, b],
                    other_core,
                )
            )
            arrivals.append((other_all.at[b, origin], over_recv.at[number, b]))

        def landed(ref, sem):
            pltpu.make_async_copy(ref, ref, sem).wait()

        def line(j, b):
            origin = cell(j, 0, 0)
            spot = mine_all.at[b, origin]
            if j:
                landed(spot, z_recv.at[j, b])
            src = spot if j else mine.at[slot(b)]
            start(remote(src, spot, one_send.at[j, b], one_recv.at[j, b], first(b)[0]))
            start(remote(src, spot, two_send.at[j, b, 0], two_recv.at[j, b, 0], second(b)[0]))
            if j:
                across(origin, b, j)

        def once(j, b):
            _, ty, tx = first(b)
            origin = cell(j, ty, tx)
            spot = mine_all.at[b, origin]
            landed(spot, one_recv.at[j, b])
            start(remote(spot, spot, two_send.at[j, b, 1], two_recv.at[j, b, 1], second(b)[0]))
            across(origin, b, 4 + j)

        def twice(j, b):
            _, ty, tx = second(b)
            for which, origin in enumerate((cell(j, ty, tx), cell(j, 1, 1))):
                landed(mine_all.at[b, origin], two_recv.at[j, b, which])
                across(origin, b, 8 + 2 * j + which)

        for b in (1, 0):
            line(0, b)
        for j in (1, 3, 2):
            for b in (1, 0):
                spot = mine_all.at[b, p]
                start(remote(mine.at[slot(b)], spot, z_send.at[j, b], z_recv.at[j, b], over_z[j]))
        for c in rims:
            c.start()
        for act, j in (
            (once, 0),
            (line, 1),
            (line, 3),
            (once, 1),
            (twice, 0),
            (line, 2),
            (once, 3),
            (twice, 1),
            (once, 2),
            (twice, 3),
            (twice, 2),
        ):
            for b in (1, 0):
                act(j, b)
        for c in rims:
            c.wait()
        for ref, sem in arrivals:
            landed(ref, sem)
        for c in pending:
            c.wait_send()

    def own(slot):
        copies = []
        for b in (0, 1):
            copies.append(pltpu.make_async_copy(win.at[slot(b)], win_all.at[b, p], own_sem.at[0, b]))
            copies.append(
                pltpu.make_async_copy(wout.at[slot(b)], wout_all.at[b, p], own_sem.at[1, b])
            )
        return copies

    @pl.when(core == 0)
    def _():
        for c in own(lambda b: b):
            c.start()
        carry(win, win_all, wout_all, lambda b: b)
        for c in own(lambda b: b):
            c.wait()

    @pl.when(core == 1)
    def _():
        for c in own(lambda b: 1 - b):
            c.start()
        carry(wout, wout_all, win_all, lambda b: 1 - b)
        for c in own(lambda b: 1 - b):
            c.wait()


def gathered(w_in, w_out, x_down, x_up, width):
    n = lax.axis_size("space")
    p = lax.axis_index("space")
    win, wout = w_in[0], w_out[0]
    dma = pltpu.SemaphoreType.DMA
    rim = jax.ShapeDtypeStruct((2, width) + x_up.shape[1:], x_up.dtype)
    win_all, wout_all, above, below = pl.pallas_call(
        gather_kernel,
        out_shape=(
            jax.ShapeDtypeStruct((2, n) + win.shape[1:], win.dtype),
            jax.ShapeDtypeStruct((2, n) + wout.shape[1:], wout.dtype),
            rim,
            rim,
        ),
        in_specs=[pl.BlockSpec(memory_space=pl.ANY)] * 4,
        out_specs=(pl.BlockSpec(memory_space=pl.ANY),) * 4,
        scratch_shapes=[
            dma((2, 2)),
            dma((4, 2)),
            dma((4, 2)),
            dma((4, 2)),
            dma((4, 2)),
            dma((4, 2, 2)),
            dma((4, 2, 2)),
            dma((16, 2)),
            dma((16, 2)),
            dma((2, 2)),
            dma((2, 2)),
        ],
        compiler_params=pltpu.CompilerParams(collective_id=0, has_side_effects=True),
        name="gather_weights",
    )(win, wout, x_down, x_up)
    above = jnp.where(p == 0, jnp.zeros_like(above), above)
    below = jnp.where(p == n - 1, jnp.zeros_like(below), below)
    return (
        win_all.reshape(2, n * win.shape[1], win.shape[2]),
        wout_all.reshape(2, n * wout.shape[1], wout.shape[2]),
        [
            jnp.concatenate([above[m], x, below[m]], axis=0)
            for m, x in enumerate((x_down, x_up))
        ],
    )


def sum_kernel(
    part,
    dk,
    out,
    dk_out,
    sa1,
    sb1,
    ra1,
    rb1,
    sa2,
    sb2,
    ra2,
    rb2,
    s3,
    r3,
    kr1,
    ks2,
    kr2,
    ks3,
    kr3,
    send_sem,
    recv_sem,
):
    core = lax.axis_index("segment")
    p = lax.axis_index("space")
    z = p // 4
    y = (p // 2) % 2
    x = p % 2
    half = out.shape[0] // 2
    over_x = (core, z * 4 + y * 2 + 1 - x)
    over_y = (core, z * 4 + (1 - y) * 2 + x)
    over_z = [(core, ((z + j) % 4) * 4 + y * 2 + x) for j in (1, 2, 3)]
    barrier = pltpu.get_barrier_semaphore()
    for device in [over_x, over_y] + over_z:
        pl.semaphore_signal(barrier, inc=1, device_id=device, device_id_type=MESH)

    def sent(src, dst, number, device):
        return pltpu.make_async_remote_copy(
            src_ref=src,
            dst_ref=dst,
            send_sem=send_sem.at[number],
            recv_sem=recv_sem.at[number],
            device_id=device,
            device_id_type=MESH,
        )

    low, high = pl.ds(0, half), pl.ds(half, half)
    for zz in range(4):
        for o in range(2):
            sa1[zz, o] = part[zz, o, 1 - x, low].astype(sa1.dtype)
            sb1[zz, o] = part[zz, 1 - y, o, high].astype(sb1.dtype)
    pl.semaphore_wait(barrier, 5)
    first = [sent(sa1, ra1, 0, over_x), sent(sb1, rb1, 1, over_y), sent(dk, kr1, 2, over_x)]
    for c in first:
        c.start()
    for c in first:
        c.wait_recv()
    for zz in range(4):
        sa2[zz] = (part[zz, 1 - y, x, low] + ra1[zz, 1 - y].astype(jnp.float32)).astype(sa2.dtype)
        sb2[zz] = (part[zz, y, 1 - x, high] + rb1[zz, 1 - x].astype(jnp.float32)).astype(sb2.dtype)
    ks2[...] = dk[...] + kr1[...]
    second = [sent(sa2, ra2, 3, over_y), sent(sb2, rb2, 4, over_x), sent(ks2, kr2, 5, over_y)]
    for c in second:
        c.start()

    def kept(zz):
        a = part[zz, y, x, low] + ra1[zz, y].astype(jnp.float32)
        b = part[zz, y, x, high] + rb1[zz, x].astype(jnp.float32)
        return a, b

    for c in second:
        c.wait_recv()
    ksum = ks2[...] + kr2[...]
    ks3[...] = ksum.astype(ks3.dtype)
    third = []
    for j in (1, 2, 3):
        zz = (z + j) % 4
        a, b = kept(zz)
        s3[j - 1, low] = (a + ra2[zz].astype(jnp.float32)).astype(s3.dtype)
        s3[j - 1, high] = (b + rb2[zz].astype(jnp.float32)).astype(s3.dtype)
        third.append(sent(s3.at[j - 1], r3.at[j - 1], 6 + j, over_z[j - 1]))
        third.append(sent(ks3, kr3.at[j - 1], 9 + j, over_z[j - 1]))
        third[-2].start()
        third[-1].start()
    a, b = kept(z)
    a = a + ra2[z].astype(jnp.float32)
    b = b + rb2[z].astype(jnp.float32)
    for c in third:
        c.wait_recv()
    for j in range(3):
        a = a + r3[j, low].astype(jnp.float32)
        b = b + r3[j, high].astype(jnp.float32)
        ksum = ksum + kr3[j].astype(jnp.float32)
    out[low] = a
    out[high] = b
    dk_out[...] = ksum
    for c in first + second + third:
        c.wait_send()


def summed(part, dk):
    n = lax.axis_size("space")
    share, chans = part.shape[0] // n, part.shape[1]
    part = part.reshape(4, 2, 2, share, chans)
    taps = dk.shape[0]
    dk = jnp.pad(dk, ((0, -taps % 16), (0, 0)))
    half = share // 2
    sent = jnp.bfloat16
    wide = pltpu.VMEM((4, 2, half, chans), sent)
    narrow = pltpu.VMEM((4, half, chans), sent)
    out, dk = pl.pallas_call(
        sum_kernel,
        out_shape=(
            jax.ShapeDtypeStruct((share, chans), jnp.float32),
            jax.ShapeDtypeStruct(dk.shape, jnp.float32),
        ),
        in_specs=[pl.BlockSpec(memory_space=pltpu.VMEM)] * 2,
        out_specs=(pl.BlockSpec(memory_space=pltpu.VMEM),) * 2,
        scratch_shapes=[
            wide,
            wide,
            wide,
            wide,
            narrow,
            narrow,
            narrow,
            narrow,
            pltpu.VMEM((3, share, chans), sent),
            pltpu.VMEM((3, share, chans), sent),
            pltpu.VMEM(dk.shape, jnp.float32),
            pltpu.VMEM(dk.shape, jnp.float32),
            pltpu.VMEM(dk.shape, jnp.float32),
            pltpu.VMEM(dk.shape, sent),
            pltpu.VMEM((3,) + dk.shape, sent),
            pltpu.SemaphoreType.DMA((13,)),
            pltpu.SemaphoreType.DMA((13,)),
        ],
        compiler_params=pltpu.CompilerParams(
            collective_id=1, has_side_effects=True, vmem_limit_bytes=24 * 1024 * 1024
        ),
        name="sum_gradients",
    )(part, dk)
    return out, dk[:taps]


def padded_2(cells, sides, width):
    for axis, dim in sides:
        count = lax.axis_size(axis)
        ends = count - 1
        head = lax.slice_in_dim(cells, 0, width, axis=dim)
        tail = lax.slice_in_dim(cells, cells.shape[dim] - width, cells.shape[dim], axis=dim)
        cells = jnp.concatenate(
            [
                lax.ppermute(tail, axis, [(i, (i + 1) % count) for i in range(ends)]),
                cells,
                lax.ppermute(head, axis, [((i + 1) % count, i) for i in range(ends)]),
            ],
            axis=dim,
        )
    return cells


def passed_along(shard, axis, by):
    devices = lax.axis_size(axis)
    pairs = [(i, i + by) for i in range(devices) if 0 <= i + by < devices]
    return lax.ppermute(shard, axis, pairs)


def as_sent(shard):
    return jax.tree.map(lambda a: a.astype(jnp.bfloat16) if a.dtype == jnp.float32 else a, shard)


def swapped(block, axis, stride):
    count = lax.axis_size(axis)
    route = []
    for low in range(count):
        high = low | 1 << stride
        if high != low and high < count:
            route += [(low, high), (high, low)]
    return lax.ppermute(block, axis, route)


def gelu_parts(a):
    inner = 0.7978845608 * (a + 0.044715 * a * a * a)
    th = jnp.tanh(inner)
    value = 0.5 * a * (1.0 + th)
    slope = 0.5 * (1.0 + th) + 0.5 * a * (1.0 - th * th) * 0.7978845608 * (1.0 + 0.134145 * a * a)
    return (value, slope)


def grouped_conv(padded, filters):
    chans = padded.shape[2]
    result = lax.conv_general_dilated(
        padded[None],
        filters,
        (1, 1),
        "VALID",
        dimension_numbers=("NHWC", "HWIO", "NHWC"),
        feature_group_count=chans,
        precision=lax.Precision.HIGHEST,
    )
    return result[0]


def depthwise(padded, kernel):
    chans = kernel.shape[1]
    filters = kernel.reshape(KSIDE, KSIDE, 1, chans)
    return grouped_conv(padded, filters)


def depthwise_back(padded, kernel):
    chans = kernel.shape[1]
    filters = kernel.reshape(KSIDE, KSIDE, 1, chans)[::-1, ::-1]
    return grouped_conv(padded, filters)


def kernel_terms(padded, grad):
    rows, cols, chans = grad.shape
    filters = grad.reshape(rows, cols, 1, chans)
    return grouped_conv(padded, filters).reshape(KSIDE * KSIDE, chans)


def pointwise_back(v, g, gain, bias, w_first, b_first, w_second, scale_res):
    rows, cols, chans = v.shape
    flat = v.reshape(rows * cols, chans)
    mean_v = jnp.mean(flat, axis=1, keepdims=True)
    centred = flat - mean_v
    rs = lax.rsqrt(jnp.mean(centred * centred, axis=1, keepdims=True) + 1e-06)
    nh = centred * rs
    normed = (nh * gain + bias).astype(jnp.bfloat16)
    pre = jnp.dot(normed, w_first, preferred_element_type=jnp.float32) + b_first
    value, slope = gelu_parts(pre)
    hidden = value.astype(jnp.bfloat16)
    outer = (g.reshape(rows * cols, chans).astype(jnp.float32) * scale_res).astype(jnp.bfloat16)
    dh = lax.dot_general(
        outer, w_second, (((1,), (1,)), ((), ())), preferred_element_type=jnp.float32
    )
    da = (dh * slope).astype(jnp.bfloat16)
    dn = lax.dot_general(da, w_first, (((1,), (1,)), ((), ())), preferred_element_type=jnp.float32)
    q = dn * gain
    du = rs * (
        q - jnp.mean(q, axis=1, keepdims=True) - nh * jnp.mean(q * nh, axis=1, keepdims=True)
    )
    return (du.astype(jnp.bfloat16).reshape(rows, cols, chans), hidden, outer)


def front_kernel(v, g, gain, bias, w_first, b_first, w_second, scale_res, du, hidden, outer):
    du[...], hidden[...], outer[...] = pointwise_back(
        v[...], g[...], gain[...], bias[...], w_first[...], b_first[...], w_second[...], scale_res[...]
    )


def front_by_kernel(v, g, gain, bias, w_first, b_first, w_second, scale_res):
    rows, cols, chans = v.shape
    units = w_first.shape[1]
    vmem = pl.BlockSpec(memory_space=pltpu.VMEM)
    return pl.pallas_call(
        front_kernel,
        out_shape=(
            jax.ShapeDtypeStruct(v.shape, jnp.bfloat16),
            jax.ShapeDtypeStruct((rows * cols, units), jnp.bfloat16),
            jax.ShapeDtypeStruct((rows * cols, chans), jnp.bfloat16),
        ),
        in_specs=[vmem] * 8,
        out_specs=(vmem,) * 3,
        compiler_params=pltpu.CompilerParams(vmem_limit_bytes=24 * 1024 * 1024),
        cost_estimate=pl.CostEstimate(
            flops=6 * rows * cols * chans * units,
            bytes_accessed=4 * chans * units + 12 * rows * cols * chans,
            transcendentals=rows * cols * units,
        ),
        name="pointwise_layers",
    )(v, g, gain[None], bias[None], w_first, b_first[None], w_second, scale_res[None])


def per_device(
    stash_down,
    stash_up,
    grad_down,
    grad_up,
    dw_kernel,
    norm_gain,
    norm_bias,
    w_in,
    b_in,
    w_out,
    layer_scale,
):
    segments = lax.axis_size("segment")
    me = lax.axis_index("segment")
    half = KSIDE // 2
    rows, cols, chans = (stash_down.shape[1], stash_down.shape[2], stash_down.shape[3])
    hidden_units = w_in.shape[3]
    norm = 1.0 / math.sqrt(2.0 * rows * lax.axis_size("space") * cols)
    paired = segments == 2 and lax.axis_size("space") == 16
    if paired:
        w_in_all, w_out_all, rimmed_both = gathered(
            w_in, w_out, stash_down[0], stash_up[0], half
        )
    else:
        w_in_all, w_out_all = (
            lax.all_gather(w_in, "space", axis=2, tiled=True)[0],
            lax.all_gather(w_out, "space", axis=2, tiled=True)[0],
        )
        both = jnp.concatenate([stash_down, stash_up])
        rimmed_both = padded_2(both, (("space", 1),), half)
    down_in = grad_down
    up_in = grad_up
    out_down = jnp.zeros_like(grad_down)
    out_up = jnp.zeros_like(grad_up)
    tokens = rows * cols
    hid_down = jnp.zeros((tokens, hidden_units), jnp.bfloat16)
    hid_up = jnp.zeros((tokens, hidden_units), jnp.bfloat16)
    outer_down = jnp.zeros((tokens, chans), jnp.bfloat16)
    outer_up = jnp.zeros((tokens, chans), jnp.bfloat16)
    kern_down = jnp.zeros((KSIDE * KSIDE, chans), jnp.float32)
    kern_up = jnp.zeros((KSIDE * KSIDE, chans), jnp.float32)
    for step in range(segments):
        on_up = me == step
        on_down = me == segments - 1 - step
        active = jnp.logical_or(on_up, on_down)
        pick = on_up.astype(jnp.int32)

        def select(array):
            return lax.dynamic_index_in_dim(array[0], pick, 0, keepdims=False)

        rimmed = jnp.where(on_up, rimmed_both[1], rimmed_both[0])
        padded = jnp.pad(rimmed.astype(jnp.float32), ((0, 0), (half, half), (0, 0)))
        g = jnp.where(on_up, up_in, down_in)
        kern = select(dw_kernel).astype(jnp.float32)

        def chosen(array):
            if paired:
                return array[segments - 1 - step]
            return lax.dynamic_index_in_dim(array, pick, 0, keepdims=False)

        def front_live():
            v = depthwise(padded, kern)
            layers = front_by_kernel if paired else pointwise_back
            return layers(
                v,
                g,
                select(norm_gain),
                select(norm_bias),
                chosen(w_in_all),
                select(b_in),
                chosen(w_out_all),
                select(layer_scale),
            )

        def front_spare():
            return (
                jnp.zeros((rows, cols, chans), jnp.bfloat16),
                jnp.zeros((tokens, hidden_units), jnp.bfloat16),
                jnp.zeros((tokens, chans), jnp.bfloat16),
            )

        du, hidden, outer = front_live() if paired else lax.cond(active, front_live, front_spare)
        du_rimmed = padded_2(du, (("space", 0),), half)

        def back_live():
            du_pad = jnp.pad(du_rimmed.astype(jnp.float32), ((0, 0), (half, half), (0, 0)))
            dx_new = (g.astype(jnp.float32) + depthwise_back(du_pad, kern)).astype(jnp.bfloat16)
            dk_new = kernel_terms(padded, du.astype(jnp.float32))
            return (dx_new, dk_new)

        def back_spare():
            return (
                jnp.zeros((rows, cols, chans), jnp.bfloat16),
                jnp.zeros((KSIDE * KSIDE, chans), jnp.float32),
            )

        dx, dk = back_live() if paired else lax.cond(active, back_live, back_spare)
        out_down = jnp.where(on_down, dx, out_down)
        out_up = jnp.where(on_up, dx, out_up)
        kern_down = jnp.where(on_down, dk, kern_down)
        kern_up = jnp.where(on_up, dk, kern_up)
        hid_down = jnp.where(on_down, hidden, hid_down)
        hid_up = jnp.where(on_up, hidden, hid_up)
        outer_down = jnp.where(on_down, outer, outer_down)
        outer_up = jnp.where(on_up, outer, outer_up)
        if paired and step == 0:
            down_in = up_in = swapped(dx, "segment", 0)
        elif step + 1 < segments:
            down_in = passed_along(dx, "segment", -1)
            up_in = passed_along(dx, "segment", 1)
    levels = segments.bit_length() - 1
    for bit in range(levels):
        kern_up = swapped(as_sent(kern_up), "segment", bit).astype(kern_up.dtype)
    share = w_out.shape[2]
    joined = jnp.concatenate([hid_up, outer_up], axis=1)
    for bit in range(levels):
        joined = swapped(joined, "segment", bit)
    all_hidden = jnp.concatenate([hid_down, joined[:, :hidden_units]], axis=0)
    all_outer = jnp.concatenate([outer_down, joined[:, hidden_units:]], axis=0)
    columns = lax.slice_in_dim(all_hidden, 0, share * lax.axis_size("space"), axis=1)
    w_part = (
        lax.dot_general(
            columns, all_outer, (((0,), (0,)), ((), ())), preferred_element_type=jnp.float32
        )
        * norm
    )
    k_part = (kern_down + kern_up) * norm
    if paired:
        w_grad, k_grad = summed(w_part, k_part)
    else:
        w_grad = lax.psum_scatter(w_part, "space", scatter_dimension=0, tiled=True)
        k_grad = lax.psum(k_part, "space")
    return (out_down[None], out_up[None], w_grad[None], k_grad[None])


def solution(mesh):
    return jax.shard_map(
        per_device,
        mesh=mesh,
        in_specs=(
            P("segment", "space", None, None),
            P("segment", "space", None, None),
            P("space", None, None),
            P("space", None, None),
            P("segment", None, None, None),
            P("segment", None, None),
            P("segment", None, None),
            P("segment", None, "space", None),
            P("segment", None, None),
            P("segment", None, "space", None),
            P("segment", None, None),
        ),
        out_specs=(
            P("segment", "space", None, None),
            P("segment", "space", None, None),
            P("segment", "space", None),
            P("segment", None, None),
        ),
        check_vma=False,
    )
```

```python
import functools
import math

import jax
import jax.numpy as jnp
from jax import lax
from jax.experimental import pallas as pl
from jax.experimental.pallas import tpu as pltpu
from jax.sharding import PartitionSpec as P

KSIDE = 7


MESH = pl.DeviceIdType.MESH


def gather_kernel(
    win,
    wout,
    x_down,
    x_up,
    win_all,
    wout_all,
    above,
    below,
    own_sem,
    z_send,
    z_recv,
    one_send,
    one_recv,
    two_send,
    two_recv,
    over_send,
    over_recv,
    rim_send,
    rim_recv,
):
    core = lax.axis_index("segment")
    p = lax.axis_index("space")
    z = p // 4
    y = (p // 2) % 2
    xx = p % 2
    after, before = (core, (p + 1) % 16), (core, (p + 15) % 16)
    over_x = (core, z * 4 + y * 2 + 1 - xx)
    over_y = (core, z * 4 + (1 - y) * 2 + xx)
    over_z = {j: (core, ((z + j) % 4) * 4 + y * 2 + xx) for j in (1, 2, 3)}
    other_core = (1 - core, p)
    barrier = pltpu.get_barrier_semaphore()
    greeted = [over_x, over_y, other_core, after, before] + list(over_z.values())
    for device in greeted:
        pl.semaphore_signal(barrier, inc=1, device_id=device, device_id_type=MESH)
    pl.semaphore_wait(barrier, len(greeted))

    def remote(src, dst, send, recv, device):
        return pltpu.make_async_remote_copy(
            src_ref=src,
            dst_ref=dst,
            send_sem=send,
            recv_sem=recv,
            device_id=device,
            device_id_type=MESH,
        )

    width, rows = above.shape[1], x_up.shape[0]
    rims = []
    for m, x in enumerate((x_down, x_up)):
        rims.append(
            remote(
                x.at[pl.ds(rows - width, width)],
                above.at[m],
                rim_send.at[m, 0],
                rim_recv.at[m, 0],
                after,
            )
        )
        rims.append(
            remote(
                x.at[pl.ds(0, width)], below.at[m], rim_send.at[m, 1], rim_recv.at[m, 1], before
            )
        )

    def carry(mine, mine_all, other_all, slot):
        def cell(j, turned_y, turned_x):
            yy = 1 - y if turned_y else y
            xo = 1 - xx if turned_x else xx
            return ((z + 4 - j) % 4) * 4 + yy * 2 + xo

        def first(b):
            return (over_x, 0, 1) if b == 1 else (over_y, 1, 0)

        def second(b):
            return (over_y, 1, 0) if b == 1 else (over_x, 0, 1)

        pending = []

        def start(copy):
            copy.start()
            pending.append(copy)

        arrivals = []

        def across(origin, b, number):
            start(
                remote(
                    mine_all.at[b, origin],
                    mine_all.at[b, origin],
                    over_send.at[number, b],
                    over_recv.at[number, b],
                    other_core,
                )
            )
            arrivals.append((other_all.at[b, origin], over_recv.at[number, b]))

        def landed(ref, sem):
            pltpu.make_async_copy(ref, ref, sem).wait()

        def line(j, b):
            origin = cell(j, 0, 0)
            spot = mine_all.at[b, origin]
            if j:
                landed(spot, z_recv.at[j, b])
            src = spot if j else mine.at[slot(b)]
            start(remote(src, spot, one_send.at[j, b], one_recv.at[j, b], first(b)[0]))
            start(remote(src, spot, two_send.at[j, b, 0], two_recv.at[j, b, 0], second(b)[0]))
            if j:
                across(origin, b, j)

        def once(j, b):
            _, ty, tx = first(b)
            origin = cell(j, ty, tx)
            spot = mine_all.at[b, origin]
            landed(spot, one_recv.at[j, b])
            start(remote(spot, spot, two_send.at[j, b, 1], two_recv.at[j, b, 1], second(b)[0]))
            across(origin, b, 4 + j)

        def twice(j, b):
            _, ty, tx = second(b)
            for which, origin in enumerate((cell(j, ty, tx), cell(j, 1, 1))):
                landed(mine_all.at[b, origin], two_recv.at[j, b, which])
                across(origin, b, 8 + 2 * j + which)

        for b in (1, 0):
            line(0, b)
        for j in (1, 3, 2):
            for b in (1, 0):
                spot = mine_all.at[b, p]
                start(remote(mine.at[slot(b)], spot, z_send.at[j, b], z_recv.at[j, b], over_z[j]))
        for c in rims:
            c.start()
        for act, j in (
            (once, 0),
            (line, 1),
            (line, 3),
            (once, 1),
            (twice, 0),
            (line, 2),
            (once, 3),
            (twice, 1),
            (once, 2),
            (twice, 3),
            (twice, 2),
        ):
            for b in (1, 0):
                act(j, b)
        for c in rims:
            c.wait()
        for ref, sem in arrivals:
            landed(ref, sem)
        for c in pending:
            c.wait_send()

    def own(slot):
        copies = []
        for b in (0, 1):
            copies.append(pltpu.make_async_copy(win.at[slot(b)], win_all.at[b, p], own_sem.at[0, b]))
            copies.append(
                pltpu.make_async_copy(wout.at[slot(b)], wout_all.at[b, p], own_sem.at[1, b])
            )
        return copies

    @pl.when(core == 0)
    def _():
        for c in own(lambda b: b):
            c.start()
        carry(win, win_all, wout_all, lambda b: b)
        for c in own(lambda b: b):
            c.wait()

    @pl.when(core == 1)
    def _():
        for c in own(lambda b: 1 - b):
            c.start()
        carry(wout, wout_all, win_all, lambda b: 1 - b)
        for c in own(lambda b: 1 - b):
            c.wait()


def gathered(w_in, w_out, x_down, x_up, width):
    n = lax.axis_size("space")
    p = lax.axis_index("space")
    win, wout = w_in[0], w_out[0]
    dma = pltpu.SemaphoreType.DMA
    rim = jax.ShapeDtypeStruct((2, width) + x_up.shape[1:], x_up.dtype)
    win_all, wout_all, above, below = pl.pallas_call(
        gather_kernel,
        out_shape=(
            jax.ShapeDtypeStruct((2, n) + win.shape[1:], win.dtype),
            jax.ShapeDtypeStruct((2, n) + wout.shape[1:], wout.dtype),
            rim,
            rim,
        ),
        in_specs=[pl.BlockSpec(memory_space=pl.ANY)] * 4,
        out_specs=(pl.BlockSpec(memory_space=pl.ANY),) * 4,
        scratch_shapes=[
            dma((2, 2)),
            dma((4, 2)),
            dma((4, 2)),
            dma((4, 2)),
            dma((4, 2)),
            dma((4, 2, 2)),
            dma((4, 2, 2)),
            dma((16, 2)),
            dma((16, 2)),
            dma((2, 2)),
            dma((2, 2)),
        ],
        compiler_params=pltpu.CompilerParams(collective_id=0, has_side_effects=True),
        name="gather_weights",
    )(win, wout, x_down, x_up)
    above = jnp.where(p == 0, jnp.zeros_like(above), above)
    below = jnp.where(p == n - 1, jnp.zeros_like(below), below)
    return (
        win_all.reshape(2, n * win.shape[1], win.shape[2]),
        wout_all.reshape(2, n * wout.shape[1], wout.shape[2]),
        [
            jnp.concatenate([above[m], x, below[m]], axis=0)
            for m, x in enumerate((x_down, x_up))
        ],
    )


def sum_kernel(
    part,
    dk,
    out,
    dk_out,
    sa1,
    sb1,
    ra1,
    rb1,
    sa2,
    sb2,
    ra2,
    rb2,
    s3,
    r3,
    kr1,
    ks2,
    kr2,
    ks3,
    kr3,
    send_sem,
    recv_sem,
):
    core = lax.axis_index("segment")
    p = lax.axis_index("space")
    z = p // 4
    y = (p // 2) % 2
    x = p % 2
    half = out.shape[0] // 2
    over_x = (core, z * 4 + y * 2 + 1 - x)
    over_y = (core, z * 4 + (1 - y) * 2 + x)
    over_z = [(core, ((z + j) % 4) * 4 + y * 2 + x) for j in (1, 2, 3)]
    barrier = pltpu.get_barrier_semaphore()
    for device in [over_x, over_y] + over_z:
        pl.semaphore_signal(barrier, inc=1, device_id=device, device_id_type=MESH)

    def sent(src, dst, number, device):
        return pltpu.make_async_remote_copy(
            src_ref=src,
            dst_ref=dst,
            send_sem=send_sem.at[number],
            recv_sem=recv_sem.at[number],
            device_id=device,
            device_id_type=MESH,
        )

    low, high = pl.ds(0, half), pl.ds(half, half)
    order = (1, 3, 2, 0)
    at = [(z + j) % 4 for j in range(4)]
    first, second, third = {}, {}, []
    waited = False
    for j in order:
        for o in range(2):
            sa1[j, o] = part[at[j], o, 1 - x, low].astype(sa1.dtype)
            sb1[j, o] = part[at[j], 1 - y, o, high].astype(sb1.dtype)
        if not waited:
            pl.semaphore_wait(barrier, 5)
            waited = True
        first[j] = (
            sent(sa1.at[j], ra1.at[j], j, over_x),
            sent(sb1.at[j], rb1.at[j], 4 + j, over_y),
        )
        for c in first[j]:
            c.start()
    dk_first = sent(dk, kr1, 22, over_x)
    dk_first.start()
    for j in order:
        for c in first[j]:
            c.wait_recv()
        sa2[j] = (part[at[j], 1 - y, x, low] + ra1[j, 1 - y].astype(jnp.float32)).astype(sa2.dtype)
        sb2[j] = (part[at[j], y, 1 - x, high] + rb1[j, 1 - x].astype(jnp.float32)).astype(sb2.dtype)
        second[j] = (
            sent(sa2.at[j], ra2.at[j], 8 + j, over_y),
            sent(sb2.at[j], rb2.at[j], 12 + j, over_x),
        )
        for c in second[j]:
            c.start()
    dk_first.wait_recv()
    ks2[...] = dk[...] + kr1[...]
    dk_second = sent(ks2, kr2, 23, over_y)
    dk_second.start()

    def kept(j):
        for c in second[j]:
            c.wait_recv()
        a = part[at[j], y, x, low] + ra1[j, y].astype(jnp.float32)
        b = part[at[j], y, x, high] + rb1[j, x].astype(jnp.float32)
        return a + ra2[j].astype(jnp.float32), b + rb2[j].astype(jnp.float32)

    for j in (1, 3, 2):
        a, b = kept(j)
        s3[j - 1, low] = a.astype(s3.dtype)
        s3[j - 1, high] = b.astype(s3.dtype)
        third.append(sent(s3.at[j - 1], r3.at[j - 1], 15 + j, over_z[j - 1]))
        third[-1].start()
    a, b = kept(0)
    dk_second.wait_recv()
    ksum = ks2[...] + kr2[...]
    ks3[...] = ksum.astype(ks3.dtype)
    for j in (1, 3, 2):
        third.append(sent(ks3, kr3.at[j - 1], 18 + j, over_z[j - 1]))
        third[-1].start()
    for c in third:
        c.wait_recv()
    for j in range(3):
        a = a + r3[j, low].astype(jnp.float32)
        b = b + r3[j, high].astype(jnp.float32)
        ksum = ksum + kr3[j].astype(jnp.float32)
    out[low] = a
    out[high] = b
    dk_out[...] = ksum
    for j in order:
        for c in first[j] + second[j]:
            c.wait_send()
    for c in [dk_first, dk_second] + third:
        c.wait_send()


def summed(part, dk):
    n = lax.axis_size("space")
    share, chans = part.shape[0] // n, part.shape[1]
    part = part.reshape(4, 2, 2, share, chans)
    taps = dk.shape[0]
    dk = jnp.pad(dk, ((0, -taps % 16), (0, 0)))
    half = share // 2
    sent = jnp.bfloat16
    wide = pltpu.VMEM((4, 2, half, chans), sent)
    narrow = pltpu.VMEM((4, half, chans), sent)
    out, dk = pl.pallas_call(
        sum_kernel,
        out_shape=(
            jax.ShapeDtypeStruct((share, chans), jnp.float32),
            jax.ShapeDtypeStruct(dk.shape, jnp.float32),
        ),
        in_specs=[pl.BlockSpec(memory_space=pltpu.VMEM)] * 2,
        out_specs=(pl.BlockSpec(memory_space=pltpu.VMEM),) * 2,
        scratch_shapes=[
            wide,
            wide,
            wide,
            wide,
            narrow,
            narrow,
            narrow,
            narrow,
            pltpu.VMEM((3, share, chans), sent),
            pltpu.VMEM((3, share, chans), sent),
            pltpu.VMEM(dk.shape, jnp.float32),
            pltpu.VMEM(dk.shape, jnp.float32),
            pltpu.VMEM(dk.shape, jnp.float32),
            pltpu.VMEM(dk.shape, sent),
            pltpu.VMEM((3,) + dk.shape, sent),
            pltpu.SemaphoreType.DMA((24,)),
            pltpu.SemaphoreType.DMA((24,)),
        ],
        compiler_params=pltpu.CompilerParams(
            collective_id=1, has_side_effects=True, vmem_limit_bytes=24 * 1024 * 1024
        ),
        name="sum_gradients",
    )(part, dk)
    return out, dk[:taps]


def padded_2(cells, sides, width):
    for axis, dim in sides:
        count = lax.axis_size(axis)
        ends = count - 1
        head = lax.slice_in_dim(cells, 0, width, axis=dim)
        tail = lax.slice_in_dim(cells, cells.shape[dim] - width, cells.shape[dim], axis=dim)
        cells = jnp.concatenate(
            [
                lax.ppermute(tail, axis, [(i, (i + 1) % count) for i in range(ends)]),
                cells,
                lax.ppermute(head, axis, [((i + 1) % count, i) for i in range(ends)]),
            ],
            axis=dim,
        )
    return cells


def passed_along(shard, axis, by):
    devices = lax.axis_size(axis)
    pairs = [(i, i + by) for i in range(devices) if 0 <= i + by < devices]
    return lax.ppermute(shard, axis, pairs)


def as_sent(shard):
    return jax.tree.map(lambda a: a.astype(jnp.bfloat16) if a.dtype == jnp.float32 else a, shard)


def swapped(block, axis, stride):
    count = lax.axis_size(axis)
    route = []
    for low in range(count):
        high = low | 1 << stride
        if high != low and high < count:
            route += [(low, high), (high, low)]
    return lax.ppermute(block, axis, route)


def gelu_parts(a):
    inner = 0.7978845608 * (a + 0.044715 * a * a * a)
    th = jnp.tanh(inner)
    value = 0.5 * a * (1.0 + th)
    slope = 0.5 * (1.0 + th) + 0.5 * a * (1.0 - th * th) * 0.7978845608 * (1.0 + 0.134145 * a * a)
    return (value, slope)


def grouped_conv(padded, filters):
    chans = padded.shape[2]
    result = lax.conv_general_dilated(
        padded[None],
        filters,
        (1, 1),
        "VALID",
        dimension_numbers=("NHWC", "HWIO", "NHWC"),
        feature_group_count=chans,
        precision=lax.Precision.HIGHEST,
    )
    return result[0]


def depthwise(padded, kernel):
    chans = kernel.shape[1]
    filters = kernel.reshape(KSIDE, KSIDE, 1, chans)
    return grouped_conv(padded, filters)


def depthwise_back(padded, kernel):
    chans = kernel.shape[1]
    filters = kernel.reshape(KSIDE, KSIDE, 1, chans)[::-1, ::-1]
    return grouped_conv(padded, filters)


def kernel_terms(padded, grad):
    rows, cols, chans = grad.shape
    filters = grad.reshape(rows, cols, 1, chans)
    return grouped_conv(padded, filters).reshape(KSIDE * KSIDE, chans)


def pointwise_back(v, g, gain, bias, w_first, b_first, w_second, scale_res):
    rows, cols, chans = v.shape
    flat = v.reshape(rows * cols, chans)
    mean_v = jnp.mean(flat, axis=1, keepdims=True)
    centred = flat - mean_v
    rs = lax.rsqrt(jnp.mean(centred * centred, axis=1, keepdims=True) + 1e-06)
    nh = centred * rs
    normed = (nh * gain + bias).astype(jnp.bfloat16)
    pre = jnp.dot(normed, w_first, preferred_element_type=jnp.float32) + b_first
    value, slope = gelu_parts(pre)
    hidden = value.astype(jnp.bfloat16)
    outer = (g.reshape(rows * cols, chans).astype(jnp.float32) * scale_res).astype(jnp.bfloat16)
    dh = lax.dot_general(
        outer, w_second, (((1,), (1,)), ((), ())), preferred_element_type=jnp.float32
    )
    da = (dh * slope).astype(jnp.bfloat16)
    dn = lax.dot_general(da, w_first, (((1,), (1,)), ((), ())), preferred_element_type=jnp.float32)
    q = dn * gain
    du = rs * (
        q - jnp.mean(q, axis=1, keepdims=True) - nh * jnp.mean(q * nh, axis=1, keepdims=True)
    )
    return (du.astype(jnp.bfloat16).reshape(rows, cols, chans), hidden, outer)


def front_kernel(v, g, gain, bias, w_first, b_first, w_second, scale_res, du, hidden, outer):
    du[...], hidden[...], outer[...] = pointwise_back(
        v[...], g[...], gain[...], bias[...], w_first[...], b_first[...], w_second[...], scale_res[...]
    )


def front_by_kernel(v, g, gain, bias, w_first, b_first, w_second, scale_res):
    rows, cols, chans = v.shape
    units = w_first.shape[1]
    vmem = pl.BlockSpec(memory_space=pltpu.VMEM)
    return pl.pallas_call(
        front_kernel,
        out_shape=(
            jax.ShapeDtypeStruct(v.shape, jnp.bfloat16),
            jax.ShapeDtypeStruct((rows * cols, units), jnp.bfloat16),
            jax.ShapeDtypeStruct((rows * cols, chans), jnp.bfloat16),
        ),
        in_specs=[vmem] * 8,
        out_specs=(vmem,) * 3,
        compiler_params=pltpu.CompilerParams(vmem_limit_bytes=24 * 1024 * 1024),
        cost_estimate=pl.CostEstimate(
            flops=6 * rows * cols * chans * units,
            bytes_accessed=4 * chans * units + 12 * rows * cols * chans,
            transcendentals=rows * cols * units,
        ),
        name="pointwise_layers",
    )(v, g, gain[None], bias[None], w_first, b_first[None], w_second, scale_res[None])


def per_device(
    stash_down,
    stash_up,
    grad_down,
    grad_up,
    dw_kernel,
    norm_gain,
    norm_bias,
    w_in,
    b_in,
    w_out,
    layer_scale,
):
    segments = lax.axis_size("segment")
    me = lax.axis_index("segment")
    half = KSIDE // 2
    rows, cols, chans = (stash_down.shape[1], stash_down.shape[2], stash_down.shape[3])
    hidden_units = w_in.shape[3]
    norm = 1.0 / math.sqrt(2.0 * rows * lax.axis_size("space") * cols)
    paired = segments == 2 and lax.axis_size("space") == 16
    if paired:
        w_in_all, w_out_all, rimmed_both = gathered(
            w_in, w_out, stash_down[0], stash_up[0], half
        )
    else:
        w_in_all, w_out_all = (
            lax.all_gather(w_in, "space", axis=2, tiled=True)[0],
            lax.all_gather(w_out, "space", axis=2, tiled=True)[0],
        )
        both = jnp.concatenate([stash_down, stash_up])
        rimmed_both = padded_2(both, (("space", 1),), half)
    down_in = grad_down
    up_in = grad_up
    out_down = jnp.zeros_like(grad_down)
    out_up = jnp.zeros_like(grad_up)
    tokens = rows * cols
    hid_down = jnp.zeros((tokens, hidden_units), jnp.bfloat16)
    hid_up = jnp.zeros((tokens, hidden_units), jnp.bfloat16)
    outer_down = jnp.zeros((tokens, chans), jnp.bfloat16)
    outer_up = jnp.zeros((tokens, chans), jnp.bfloat16)
    kern_down = jnp.zeros((KSIDE * KSIDE, chans), jnp.float32)
    kern_up = jnp.zeros((KSIDE * KSIDE, chans), jnp.float32)
    for step in range(segments):
        on_up = me == step
        on_down = me == segments - 1 - step
        active = jnp.logical_or(on_up, on_down)
        pick = on_up.astype(jnp.int32)

        def select(array):
            return lax.dynamic_index_in_dim(array[0], pick, 0, keepdims=False)

        rimmed = jnp.where(on_up, rimmed_both[1], rimmed_both[0])
        padded = jnp.pad(rimmed.astype(jnp.float32), ((0, 0), (half, half), (0, 0)))
        g = jnp.where(on_up, up_in, down_in)
        kern = select(dw_kernel).astype(jnp.float32)

        def chosen(array):
            if paired:
                return array[segments - 1 - step]
            return lax.dynamic_index_in_dim(array, pick, 0, keepdims=False)

        def front_live():
            v = depthwise(padded, kern)
            layers = front_by_kernel if paired else pointwise_back
            return layers(
                v,
                g,
                select(norm_gain),
                select(norm_bias),
                chosen(w_in_all),
                select(b_in),
                chosen(w_out_all),
                select(layer_scale),
            )

        def front_spare():
            return (
                jnp.zeros((rows, cols, chans), jnp.bfloat16),
                jnp.zeros((tokens, hidden_units), jnp.bfloat16),
                jnp.zeros((tokens, chans), jnp.bfloat16),
            )

        du, hidden, outer = front_live() if paired else lax.cond(active, front_live, front_spare)
        du_rimmed = padded_2(du, (("space", 0),), half)

        def back_live():
            du_pad = jnp.pad(du_rimmed.astype(jnp.float32), ((0, 0), (half, half), (0, 0)))
            dx_new = (g.astype(jnp.float32) + depthwise_back(du_pad, kern)).astype(jnp.bfloat16)
            dk_new = kernel_terms(padded, du.astype(jnp.float32))
            return (dx_new, dk_new)

        def back_spare():
            return (
                jnp.zeros((rows, cols, chans), jnp.bfloat16),
                jnp.zeros((KSIDE * KSIDE, chans), jnp.float32),
            )

        dx, dk = back_live() if paired else lax.cond(active, back_live, back_spare)
        out_down = jnp.where(on_down, dx, out_down)
        out_up = jnp.where(on_up, dx, out_up)
        kern_down = jnp.where(on_down, dk, kern_down)
        kern_up = jnp.where(on_up, dk, kern_up)
        hid_down = jnp.where(on_down, hidden, hid_down)
        hid_up = jnp.where(on_up, hidden, hid_up)
        outer_down = jnp.where(on_down, outer, outer_down)
        outer_up = jnp.where(on_up, outer, outer_up)
        if paired and step == 0:
            down_in = up_in = swapped(dx, "segment", 0)
        elif step + 1 < segments:
            down_in = passed_along(dx, "segment", -1)
            up_in = passed_along(dx, "segment", 1)
    levels = segments.bit_length() - 1
    for bit in range(levels):
        kern_up = swapped(as_sent(kern_up), "segment", bit).astype(kern_up.dtype)
    share = w_out.shape[2]
    joined = jnp.concatenate([hid_up, outer_up], axis=1)
    for bit in range(levels):
        joined = swapped(joined, "segment", bit)
    all_hidden = jnp.concatenate([hid_down, joined[:, :hidden_units]], axis=0)
    all_outer = jnp.concatenate([outer_down, joined[:, hidden_units:]], axis=0)
    columns = lax.slice_in_dim(all_hidden, 0, share * lax.axis_size("space"), axis=1)
    w_part = (
        lax.dot_general(
            columns, all_outer, (((0,), (0,)), ((), ())), preferred_element_type=jnp.float32
        )
        * norm
    )
    k_part = (kern_down + kern_up) * norm
    if paired:
        w_grad, k_grad = summed(w_part, k_part)
    else:
        w_grad = lax.psum_scatter(w_part, "space", scatter_dimension=0, tiled=True)
        k_grad = lax.psum(k_part, "space")
    return (out_down[None], out_up[None], w_grad[None], k_grad[None])


def solution(mesh):
    return jax.shard_map(
        per_device,
        mesh=mesh,
        in_specs=(
            P("segment", "space", None, None),
            P("segment", "space", None, None),
            P("space", None, None),
            P("space", None, None),
            P("segment", None, None, None),
            P("segment", None, None),
            P("segment", None, None),
            P("segment", None, "space", None),
            P("segment", None, None),
            P("segment", None, "space", None),
            P("segment", None, None),
        ),
        out_specs=(
            P("segment", "space", None, None),
            P("segment", "space", None, None),
            P("segment", "space", None),
            P("segment", None, None),
        ),
        check_vma=False,
    )
```
